32 devices in a mesh: variant: 2 (over y), row: 4 (over z), col: 2 (over x), sub: 2 (over core).
Axes of the slice: x: 2, y: 2, z: 4, core: 2. Of those that a mesh axis runs over, the one named last changes fastest.
Arguments:
- charges: bfloat16 [512, 128, 128], P(('variant', 'row', 'col', 'sub')), parts along dimension 0, may hold values from -6 to 6
- adj_loads: bfloat16 [512, 128, 128], P(('variant', 'row', 'col', 'sub')), parts along dimension 0, may hold values from -6 to 6
- bases: bfloat16 [512, 32, 128], P(('variant', 'row', 'col', 'sub')), parts along dimension 0, may hold values from -0.5 to 0.5
- couplings: bfloat16 [8192, 1024], P(('variant', 'row', 'col', 'sub')), parts along dimension 0, may hold values from -0.25 to 0.25
- near_blocks: bfloat16 [1536, 128, 128], P(('variant', 'row', 'col', 'sub')), parts along dimension 0, may hold values from -0.3125 to 0.3125
- near_rows: int32 [16, 48], P(('row', 'col', 'sub')), may hold values from 0 to 31
- near_cols: int32 [16, 48], P(('row', 'col', 'sub')), may hold values from 0 to 15
- far_rows: int32 [16, 256], P(('row', 'col', 'sub')), may hold values from 0 to 15
- far_slots: int32 [16, 256], P(('row', 'col', 'sub')), may hold values from 0 to 15, as said below
- send_list: int32 [16, 8, 2], P(('row', 'col', 'sub')), may hold values from -1 to 15, as said below
Outputs:
- potentials: bfloat16 [512, 128, 128], P(('variant', 'row', 'col', 'sub')), parts along dimension 0
- adjoint_field: bfloat16 [512, 128, 128], P(('variant', 'row', 'col', 'sub')), parts along dimension 0
The draws below stay inside these ranges and needn't reach their ends.
There are 2 independent parts, one for each index of `variant`. The reference program is written for one: setup_inputs(seed, part) draws one part's arguments, and reference() takes and returns one part's arrays. A program takes and returns all parts, laid end to end along the dimension named above; an argument that names none is the same for every part. Nothing has to cross between parts.
Inputs may be any that keep to these rules, and one draw needn't show every extreme that they name: `send_list`: entry [o, p, k] is a cluster of owner o, numbered within that owner, or -1 for an empty slot; the live slots of each [o, p] come first; for each draw some peer p receives 2 live slots from every owner. `far_slots`: A far pair names slot (p, k) of its owner as p * 2 + k; the slot is live in the send_list of owner p * 2 + o % 2, and every live slot of the owner is named by one far pair or more.
All inputs are finite; a program needn't handle non-finite values.
Results may differ from the reference program's by a relative error of at most 0.005.
Values may be sent and summed in bfloat16 or wider, within the bound.
A program may use at most 384 MiB of HBM per device.

```python
import jax
import jax.numpy as jnp
from jax import lax

BLOCK = 128
RANK = 32
LOADS = 128
CLU_DEV = 16
CAP = 2
FAR_PER = 16
NEAR_PER = 3
OWNERS = 16
PEERS = 8
CLUSTERS = 256
FAR_DEV = 256
FAR_PAIRS = 4096
NEAR_DEV = 48
NEAR_PAIRS = 768
N_SUB = 2


def routing(key):
    keys = jax.random.split(key, 5)
    sub_count = OWNERS // PEERS
    counts = jax.random.randint(keys[0], (OWNERS, PEERS), 0, CAP + 1)
    full_peer = jax.random.randint(keys[1], (), 0, PEERS)
    peer_ids = jnp.arange(PEERS, dtype=jnp.int32)
    counts = jnp.where(peer_ids[None, :] == full_peer, CAP, counts)
    local_ids = jax.random.randint(keys[2], (OWNERS, PEERS, CAP), 0, CLU_DEV)
    slot_ids = jnp.arange(CAP, dtype=jnp.int32)
    live_send = slot_ids[None, None, :] < counts[:, :, None]
    send_table = jnp.where(live_send, local_ids, -1).astype(jnp.int32)
    owner_ids = jnp.arange(OWNERS, dtype=jnp.int32)
    sender = peer_ids[None, :] * sub_count + (owner_ids % sub_count)[:, None]
    group_ids = jnp.broadcast_to((owner_ids // sub_count)[:, None], (OWNERS, PEERS))
    live_recv = live_send[sender, group_ids].reshape(OWNERS, PEERS * CAP)
    order = jnp.argsort(jnp.where(live_recv, 0, 1), axis=1, stable=True)
    live_count = jnp.sum(live_recv.astype(jnp.int32), axis=1)
    positions = jnp.arange(FAR_DEV, dtype=jnp.int32)[None, :]
    extra = jax.random.randint(keys[3], (OWNERS, FAR_DEV), 0, 1 << 20) % live_count[:, None]
    chosen = jnp.where(positions < live_count[:, None], positions, extra)
    slot_table = jnp.take_along_axis(order, chosen, axis=1)
    shuffle = jnp.argsort(jax.random.randint(keys[4], (OWNERS, FAR_DEV), 0, 1 << 30), axis=1, stable=True)
    slot_table = jnp.take_along_axis(slot_table, shuffle, axis=1)
    return (send_table, slot_table.astype(jnp.int32))


def draw_send_list(key, part):
    return routing(key)[0]


def draw_far_slots(key, part):
    return routing(key)[1]


def touch_ends(values, rng, least, largest):
    longest = values.shape.index(max(values.shape))
    spots = []
    for shift in (0, 1):
        where = [jax.random.randint(jax.random.fold_in(rng, axis), (), 0, length) for axis, length in enumerate(values.shape)]
        where[longest] = (where[longest] + shift) % values.shape[longest]
        spots.append(tuple(where))
    return values.at[spots[0]].set(least).at[spots[1]].set(largest)


def level_of(own_key, dims, shards, least, top_value):
    def one(axis_at, shards_of):
        heights = jax.random.uniform(jax.random.fold_in(jax.random.fold_in(own_key, 6), axis_at), (shards_of,), jnp.float32, least / len(shards), top_value / len(shards))
        return jnp.repeat(jnp.exp(heights), dims[axis_at] // shards_of).reshape((-1,) + (1,) * (len(dims) - axis_at - 1))

    gain = one(*shards[0])
    for cut in shards[1:]:
        gain = gain * one(*cut)
    return gain


def gaussian(own_key, shape, scale, reach, shards=(), kind=jnp.bfloat16):
    loudness = level_of(own_key, shape, shards, -0.22, 0.18) if shards else 1.0
    array = jax.random.normal(own_key, shape, jnp.float32) * scale * loudness
    return jnp.minimum(jnp.maximum(array, -reach), reach).astype(kind)


def setup_inputs(seed: int = 0, part: int = 0) -> dict:
    splits = jax.random.split(jax.random.key(seed), 11)
    part_keys = jax.random.split(jax.random.fold_in(splits[10], part), 11)
    charges = gaussian(part_keys[0], (CLUSTERS, BLOCK, LOADS), 1.0, 6.0, ((0, 16),))
    adj_loads = gaussian(part_keys[1], (CLUSTERS, BLOCK, LOADS), 1.0, 6.0, ((0, 16),))
    bases = gaussian(part_keys[2], (CLUSTERS, RANK, BLOCK), BLOCK ** -0.5, 0.5, ((0, 16),))
    couplings = gaussian(part_keys[3], (FAR_PAIRS, RANK * RANK), (RANK * FAR_PER) ** -0.5, 0.25, ((0, 16),))
    near_blocks = gaussian(part_keys[4], (NEAR_PAIRS, BLOCK, BLOCK), (BLOCK * NEAR_PER) ** -0.5, 0.3125, ((0, 16),))
    near_rows = touch_ends(jax.random.randint(splits[5], (OWNERS, NEAR_DEV), 0, OWNERS // PEERS * CLU_DEV), jax.random.fold_in(splits[5], 1), 0, (OWNERS // PEERS * CLU_DEV) - 1).astype(jnp.int32)
    near_cols = touch_ends(jax.random.randint(splits[6], (OWNERS, NEAR_DEV), 0, CLU_DEV), jax.random.fold_in(splits[6], 1), 0, CLU_DEV - 1).astype(jnp.int32)
    far_rows = touch_ends(jax.random.randint(splits[7], (OWNERS, FAR_DEV), 0, CLU_DEV), jax.random.fold_in(splits[7], 1), 0, CLU_DEV - 1).astype(jnp.int32)
    far_slots = draw_far_slots(jax.random.fold_in(splits[10], 71), part)
    send_list = draw_send_list(jax.random.fold_in(splits[10], 71), part)
    return {"charges": charges, "adj_loads": adj_loads, "bases": bases, "couplings": couplings, "near_blocks": near_blocks, "near_rows": near_rows, "near_cols": near_cols, "far_rows": far_rows, "far_slots": far_slots, "send_list": send_list}


highest = lax.Precision.HIGHEST


def reference(charges, adj_loads, bases, couplings, near_blocks, near_rows, near_cols, far_rows, far_slots, send_list):
    base32 = bases.astype(jnp.float32)
    coeffs = jnp.einsum("ckb,cbr->ckr", base32, charges.astype(jnp.float32), precision=highest).astype(jnp.bfloat16).astype(jnp.float32)
    adj_coeffs = jnp.einsum("ckb,cbr->ckr", base32, adj_loads.astype(jnp.float32), precision=highest).astype(jnp.bfloat16).astype(jnp.float32)
    owner_count = far_rows.shape[0]
    capacity = send_list.shape[2]
    owner_ids = jnp.arange(owner_count, dtype=jnp.int32)
    sender = (far_slots // capacity).astype(jnp.int32) * N_SUB + (owner_ids % N_SUB)[:, None]
    slot_index = (far_slots % capacity).astype(jnp.int32)
    group_index = jnp.broadcast_to((owner_ids // N_SUB)[:, None], far_slots.shape)
    local_index = send_list[sender, group_index, slot_index]
    col_cluster = (sender * CLU_DEV + local_index).astype(jnp.int32)
    coupling4 = couplings.reshape(owner_count, FAR_DEV, RANK, RANK)

    def far_forward(inputs):
        coupling, columns, rows_local = inputs
        terms = jnp.einsum("fab,fbr->far", coupling.astype(jnp.float32), coeffs[columns], precision=highest)
        return jax.ops.segment_sum(terms, rows_local, num_segments=CLU_DEV)

    far_fwd = lax.map(far_forward, (coupling4, col_cluster, far_rows)).reshape(-1, RANK, LOADS)

    def far_adjoint(total, inputs):
        coupling, columns, rows_local, owner = inputs
        start = (owner * CLU_DEV).astype(jnp.int32)
        own = lax.dynamic_slice_in_dim(adj_coeffs, start, CLU_DEV, 0)
        terms = jnp.einsum("fab,far->fbr", coupling.astype(jnp.float32), own[rows_local], precision=highest)
        return total.at[columns].add(terms), None

    empty = jnp.zeros(adj_coeffs.shape, jnp.float32)
    far_adj, _ = lax.scan(far_adjoint, empty, (coupling4, col_cluster, far_rows, owner_ids))

    chips = owner_count // N_SUB
    span = N_SUB * CLU_DEV
    chip_blocks = near_blocks.reshape(chips, N_SUB * NEAR_DEV, BLOCK, BLOCK)
    chip_rows = near_rows.reshape(chips, N_SUB * NEAR_DEV)
    chip_cols = (near_cols + (owner_ids % N_SUB)[:, None] * CLU_DEV).astype(jnp.int32).reshape(chips, N_SUB * NEAR_DEV)
    chip_charges = charges.reshape(chips, span, BLOCK, LOADS)
    chip_loads = adj_loads.reshape(chips, span, BLOCK, LOADS)

    def near_chip(inputs):
        blocks, rows_chip, cols_chip, fields, loads_chip = inputs
        blocks32 = blocks.astype(jnp.float32)
        forward = jnp.einsum("nij,njr->nir", blocks32, fields[cols_chip].astype(jnp.float32), precision=highest)
        backward = jnp.einsum("nij,nir->njr", blocks32, loads_chip[rows_chip].astype(jnp.float32), precision=highest)
        return (jax.ops.segment_sum(forward, rows_chip, num_segments=span),
                jax.ops.segment_sum(backward, cols_chip, num_segments=span))

    near_fwd, near_adj = lax.map(near_chip, (chip_blocks, chip_rows, chip_cols, chip_charges, chip_loads))
    near_fwd = near_fwd.reshape(-1, BLOCK, LOADS)
    near_adj = near_adj.reshape(-1, BLOCK, LOADS)
    potentials = jnp.einsum("ckb,ckr->cbr", base32, far_fwd, precision=highest) + near_fwd
    adjoint_field = jnp.einsum("ckb,ckr->cbr", base32, far_adj, precision=highest) + near_adj
    return potentials.astype(jnp.bfloat16), adjoint_field.astype(jnp.bfloat16)
```

```python
import functools

import jax
import jax.numpy as jnp
from jax import lax
from jax.experimental import pallas as pl
from jax.experimental.pallas import tpu as pltpu
from jax.sharding import PartitionSpec as P

MESH = pl.DeviceIdType.MESH
f32 = jnp.float32
bf16 = jnp.bfloat16
UNROLL = 8
CHUNK = 16


def loop(count, body):
    if count <= 16:
        for step in range(count):
            body(step)
    else:

        def step_body(step, carry):
            body(step)
            return carry

        lax.fori_loop(0, count, step_body, 0)


def dot(a, b):
    return jnp.dot(a, b, preferred_element_type=f32)


def dot_t(a, b):
    return lax.dot_general(a, b, (((0,), (0,)), ((), ())), preferred_element_type=f32)


def sorted_index(keys_row, other_row, idx_ref, at):
    n = keys_row.shape[1]
    lane = lax.broadcasted_iota(jnp.int32, (n, n), 1)
    sub = lax.broadcasted_iota(jnp.int32, (n, n), 0)
    keys = jnp.broadcast_to(keys_row, (n, n))
    eye = lane == sub
    key_col = jnp.sum(jnp.where(eye, keys, 0), axis=1, keepdims=True)
    other_col = jnp.sum(
        jnp.where(eye, jnp.broadcast_to(other_row, (n, n)), 0), axis=1, keepdims=True
    )
    before = (keys < key_col) | ((keys == key_col) & (lane < sub))
    rank = jnp.sum(jnp.where(before, 1, 0), axis=1, keepdims=True)
    wide = (n, 128)
    lanes = lax.broadcasted_iota(jnp.int32, wide, 1)
    subs = lax.broadcasted_iota(jnp.int32, wide, 0)
    here = rank == lanes

    def pick(values):
        return jnp.sum(jnp.where(here, values, 0), axis=0, keepdims=True)

    idx_ref[at : at + 1, :] = pick(subs)
    idx_ref[at + 1 : at + 2, :] = pick(jnp.broadcast_to(key_col, wide))
    idx_ref[at + 2 : at + 3, :] = pick(jnp.broadcast_to(other_col, wide))
    upto = jnp.sum(jnp.where(key_col <= lanes, 1, 0), axis=0, keepdims=True)
    same = jnp.sum(jnp.where(key_col == lanes, 1, 0), axis=0, keepdims=True)
    idx_ref[at + 3 : at + 4, :] = jnp.where(same > 0, upto - 1, n)


def segment_products(product, idx, at, sums):
    n = sums.shape[0] - 1
    unroll = UNROLL if n % UNROLL == 0 else 1
    sums[n] = jnp.zeros(sums.shape[1:], f32)

    def body(step, total):
        terms = []
        for u in range(unroll):
            k = step * unroll + u
            terms.append(product(idx[at, k], idx[at + 2, k]))
        for u in range(unroll):
            k = step * unroll + u
            same = (idx[at + 1, k] == idx[at + 1, jnp.maximum(k - 1, 0)]) & (k > 0)
            total = total * jnp.where(same, 1.0, 0.0).astype(f32) + terms[u]
            sums[k] = total
        return total

    lax.fori_loop(0, n // unroll, body, jnp.zeros(sums.shape[1:], f32))


def kernel(
    dims,
    charges,
    loads,
    bases,
    couplings,
    near,
    near_rows,
    near_cols,
    far_rows,
    far_slots,
    send,
    potentials,
    adjoint,
    idx_v,
    idx,
    bases32,
    bases_perm,
    coeffs,
    out_f,
    in_f,
    out_r,
    in_r,
    adj32,
    merged,
    fwd32,
    sums_f,
    sums_a,
    all_loads,
    part_out,
    part_in,
    idx_sem,
    f_send,
    f_recv,
    r_send,
    r_recv,
    pair_send,
    pair_recv,
):
    cols = dims["col"]
    clusters, rank, block = bases.shape
    peers, cap = send.shape[1], send.shape[2]
    slots = peers * cap
    chunk = min(CHUNK, slots)
    chunks = slots // chunk
    group = block // rank
    tall = rank // group
    row, col, core = lax.axis_index("row"), lax.axis_index("col"), lax.axis_index("sub")
    me = row * cols + col
    other = 1 - core

    def peer_of(d):
        p = lax.rem(me + d, peers)
        return p, {"row": p // cols, "col": lax.rem(p, cols)}

    barrier = pltpu.get_barrier_semaphore()
    pl.semaphore_signal(barrier, inc=1, device_id={"sub": other}, device_id_type=MESH)

    def greet(step):
        _, device = peer_of(step + 1)
        pl.semaphore_signal(barrier, inc=1, device_id=device, device_id_type=MESH)

    loop(peers - 1, greet)

    sorted_index(near_rows[...], near_cols[...], idx_v, 0)
    sorted_index(near_cols[...], near_rows[...], idx_v, 4)
    idx_copy = pltpu.make_async_copy(idx_v, idx, idx_sem)
    idx_copy.start()

    bases32[...] = bases[...].astype(f32).reshape(clusters * rank, block)
    for c in range(clusters):
        parts = [bases32[pl.ds(c * rank + i, tall, stride=group), :] for i in range(group)]
        bases_perm[c] = jnp.concatenate(parts, axis=0).astype(bf16)
        coeffs[c] = dot(bases[c], charges[c]).astype(bf16)
        adj32[pl.ds(c, rank, stride=clusters), :] = dot(bases_perm[c], loads[c])

    pl.semaphore_wait(barrier, peers)
    pair_loads = pltpu.make_async_remote_copy(
        src_ref=loads,
        dst_ref=all_loads.at[pl.ds(core * clusters, clusters)],
        send_sem=pair_send.at[0],
        recv_sem=pair_recv.at[0],
        device_id={"sub": other},
        device_id_type=MESH,
    )
    pair_loads.start()

    def fill(p):
        for k in range(cap):
            out_f[p, k] = coeffs[jnp.maximum(send[0, p, k], 0)]

    loop(peers, fill)

    def far_copy(src, dst, send_sem, recv_sem, step):
        p, device = peer_of(step + 1)
        return pltpu.make_async_remote_copy(
            src_ref=src.at[p],
            dst_ref=dst.at[me],
            send_sem=send_sem.at[p],
            recv_sem=recv_sem.at[me],
            device_id=device,
            device_id_type=MESH,
        )

    def far_wait(src, dst, send_sem, recv_sem, step):
        p, device = peer_of(step + 1)
        return pltpu.make_async_remote_copy(
            src_ref=src.at[p],
            dst_ref=dst.at[p],
            send_sem=send_sem.at[p],
            recv_sem=recv_sem.at[p],
            device_id=device,
            device_id_type=MESH,
        )

    loop(peers - 1, lambda step: far_copy(out_f, in_f, f_send, f_recv, step).start())
    in_f[me] = out_f[me]

    key = far_slots[...] * clusters + far_rows[...]
    pairs = key.shape[1]
    adj_flat = adj32[...].astype(bf16)
    span = chunk * rank

    def merge(ch):
        cells = lax.broadcasted_iota(jnp.int32, (chunk * clusters, pairs), 0) + ch * (
            chunk * clusters
        )
        hot = jnp.where(cells == key, 1.0, 0.0).astype(bf16)
        cell = dot(hot, couplings[...])
        for t in range(chunk):
            tile = jnp.concatenate(
                [
                    cell[t * clusters : (t + 1) * clusters, a * block : (a + 1) * block]
                    for a in range(tall)
                ],
                axis=0,
            )
            turned = tile.T.astype(bf16)
            for i in range(group):
                merged[ch, t * rank : (t + 1) * rank, i * block : (i + 1) * block] = turned[
                    i * rank : (i + 1) * rank
                ]
        back = dot(merged[ch], adj_flat).astype(bf16)
        per = chunk // cap
        out_r[pl.ds(ch * per, per)] = back.reshape(per, cap, rank, block)

    loop(chunks, merge)
    loop(peers - 1, lambda step: far_copy(out_r, in_r, r_send, r_recv, step).start())
    in_r[me] = out_r[me]

    idx_copy.wait()
    segment_products(lambda b, t: dot(near[b], charges[t]), idx, 0, sums_f)
    for c in range(clusters):
        part_out[c] = sums_f[idx[3, other * clusters + c]].astype(bf16)
    pair_part = pltpu.make_async_remote_copy(
        src_ref=part_out,
        dst_ref=part_in,
        send_sem=pair_send.at[1],
        recv_sem=pair_recv.at[1],
        device_id={"sub": other},
        device_id_type=MESH,
    )
    pair_part.start()
    all_loads[pl.ds(core * clusters, clusters)] = loads[...]

    loop(peers - 1, lambda step: far_wait(out_f, in_f, f_send, f_recv, step).wait_recv())
    per = chunk // cap
    fwd32[...] = jnp.zeros(fwd32.shape, f32)

    def forward(ch):
        arrived = in_f[pl.ds(ch * per, per)].reshape(span, block)
        fwd32[...] += dot_t(merged[ch], arrived)

    loop(chunks, forward)

    pltpu.make_async_remote_copy(
        src_ref=loads,
        dst_ref=all_loads.at[pl.ds(other * clusters, clusters)],
        send_sem=pair_send.at[0],
        recv_sem=pair_recv.at[0],
        device_id={"sub": other},
        device_id_type=MESH,
    ).wait_recv()
    segment_products(lambda b, s: dot_t(near[b], all_loads[s]), idx, 4, sums_a)

    loop(peers - 1, lambda step: far_wait(out_r, in_r, r_send, r_recv, step).wait_recv())
    for c in range(clusters):
        if peers <= 16:
            total = jnp.zeros((rank, block), f32)
            for p in range(peers):
                for k in range(cap):
                    mine = jnp.where(send[0, p, k] == c, 1.0, 0.0).astype(f32)
                    total = total + in_r[p, k].astype(f32) * mine
        else:

            def gather(p, total):
                for k in range(cap):
                    mine = jnp.where(send[0, p, k] == c, 1.0, 0.0).astype(f32)
                    total = total + in_r[p, k].astype(f32) * mine
                return total

            total = lax.fori_loop(0, peers, gather, jnp.zeros((rank, block), f32))
        far = dot_t(bases[c], total.astype(bf16))
        adjoint[c] = (far + sums_a[idx[7, c]]).astype(bf16)

    pair_part.wait_recv()
    for c in range(clusters):
        far_c = fwd32[pl.ds(c, rank, stride=clusters), :].astype(bf16)
        far = dot_t(bases_perm[c], far_c)
        mine = sums_f[idx[3, core * clusters + c]]
        potentials[c] = (far + mine + part_in[c].astype(f32)).astype(bf16)

    pair_loads.wait_send()
    pair_part.wait_send()
    loop(peers - 1, lambda step: far_wait(out_f, in_f, f_send, f_recv, step).wait_send())
    loop(peers - 1, lambda step: far_wait(out_r, in_r, r_send, r_recv, step).wait_send())


def on_device(dims, *args):
    charges, _, bases, _, near, _, _, _, _, send = args
    clusters, block, width = charges.shape
    rank = bases.shape[1]
    blocks = near.shape[0]
    peers, cap = send.shape[1], send.shape[2]
    chunk = min(CHUNK, peers * cap)
    vmem = pl.BlockSpec(memory_space=pltpu.VMEM)
    smem = pl.BlockSpec(memory_space=pltpu.SMEM)
    dma = pltpu.SemaphoreType.DMA
    slot_shape = (peers, cap, rank, width)
    full = jax.ShapeDtypeStruct((clusters, block, width), bf16)
    return pl.pallas_call(
        functools.partial(kernel, dims),
        out_shape=(full, full),
        in_specs=[vmem] * 9 + [smem],
        out_specs=(vmem, vmem),
        scratch_shapes=[
            pltpu.VMEM((8, 128), jnp.int32),
            pltpu.SMEM((8, 128), jnp.int32),
            pltpu.VMEM((clusters * rank, block), f32),
            pltpu.VMEM((clusters, rank, block), bf16),
            pltpu.VMEM((clusters, rank, width), bf16),
            pltpu.VMEM(slot_shape, bf16),
            pltpu.VMEM(slot_shape, bf16),
            pltpu.VMEM(slot_shape, bf16),
            pltpu.VMEM(slot_shape, bf16),
            pltpu.VMEM((clusters * rank, width), f32),
            pltpu.VMEM((peers * cap // chunk, chunk * rank, clusters * rank), bf16),
            pltpu.VMEM((clusters * rank, width), f32),
            pltpu.VMEM((blocks + 1, block, width), f32),
            pltpu.VMEM((blocks + 1, block, width), f32),
            pltpu.VMEM((2 * clusters, block, width), bf16),
            pltpu.VMEM((clusters, block, width), bf16),
            pltpu.VMEM((clusters, block, width), bf16),
            dma,
            dma((peers,)),
            dma((peers,)),
            dma((peers,)),
            dma((peers,)),
            dma((2,)),
            dma((2,)),
        ],
        compiler_params=pltpu.CompilerParams(
            collective_id=0, has_side_effects=True, vmem_limit_bytes=52 * 1024 * 1024
        ),
        name="hierarchical",
    )(*args)


def solution(mesh):
    split = ("variant", "row", "col", "sub")
    owner = ("row", "col", "sub")
    in_specs = (
        P(split, None, None),
        P(split, None, None),
        P(split, None, None),
        P(split, None),
        P(split, None, None),
        P(owner, None),
        P(owner, None),
        P(owner, None),
        P(owner, None),
        P(owner, None, None),
    )
    out_specs = (P(split, None, None), P(split, None, None))
    return jax.shard_map(
        functools.partial(on_device, dict(mesh.shape)),
        mesh=mesh,
        in_specs=in_specs,
        out_specs=out_specs,
        check_vma=False,
    )
```

```python
import functools

import jax
import jax.numpy as jnp
from jax import lax
from jax.experimental import pallas as pl
from jax.experimental.pallas import tpu as pltpu
from jax.sharding import PartitionSpec as P

MESH = pl.DeviceIdType.MESH
f32 = jnp.float32
bf16 = jnp.bfloat16
UNROLL = 8
CHUNK = 16


def loop(count, body):
    if count <= 16:
        for step in range(count):
            body(step)
    else:

        def step_body(step, carry):
            body(step)
            return carry

        lax.fori_loop(0, count, step_body, 0)


def dot(a, b):
    return jnp.dot(a, b, preferred_element_type=f32)


def dot_t(a, b):
    return lax.dot_general(a, b, (((0,), (0,)), ((), ())), preferred_element_type=f32)


def sorted_index(keys_row, other_row, idx_ref, at):
    n = keys_row.shape[1]
    lane = lax.broadcasted_iota(jnp.int32, (n, n), 1)
    sub = lax.broadcasted_iota(jnp.int32, (n, n), 0)
    keys = jnp.broadcast_to(keys_row, (n, n))
    eye = lane == sub
    key_col = jnp.sum(jnp.where(eye, keys, 0), axis=1, keepdims=True)
    other_col = jnp.sum(
        jnp.where(eye, jnp.broadcast_to(other_row, (n, n)), 0), axis=1, keepdims=True
    )
    before = (keys < key_col) | ((keys == key_col) & (lane < sub))
    rank = jnp.sum(jnp.where(before, 1, 0), axis=1, keepdims=True)
    wide = (n, 128)
    lanes = lax.broadcasted_iota(jnp.int32, wide, 1)
    subs = lax.broadcasted_iota(jnp.int32, wide, 0)
    here = rank == lanes

    def pick(values):
        return jnp.sum(jnp.where(here, values, 0), axis=0, keepdims=True)

    idx_ref[at : at + 1, :] = pick(subs)
    idx_ref[at + 1 : at + 2, :] = pick(jnp.broadcast_to(key_col, wide))
    idx_ref[at + 2 : at + 3, :] = pick(jnp.broadcast_to(other_col, wide))
    upto = jnp.sum(jnp.where(key_col <= lanes, 1, 0), axis=0, keepdims=True)
    same = jnp.sum(jnp.where(key_col == lanes, 1, 0), axis=0, keepdims=True)
    idx_ref[at + 3 : at + 4, :] = jnp.where(same > 0, upto - 1, n)


def segment_products(product, idx, at, sums):
    n = sums.shape[0] - 1
    unroll = UNROLL if n % UNROLL == 0 else 1
    sums[n] = jnp.zeros(sums.shape[1:], f32)

    def body(step, total):
        terms = []
        for u in range(unroll):
            k = step * unroll + u
            terms.append(product(idx[at, k], idx[at + 2, k]))
        for u in range(unroll):
            k = step * unroll + u
            same = (idx[at + 1, k] == idx[at + 1, jnp.maximum(k - 1, 0)]) & (k > 0)
            total = total * jnp.where(same, 1.0, 0.0).astype(f32) + terms[u]
            sums[k] = total
        return total

    lax.fori_loop(0, n // unroll, body, jnp.zeros(sums.shape[1:], f32))


def kernel(
    dims,
    charges_hbm,
    loads_hbm,
    bases_hbm,
    couplings_hbm,
    near_hbm,
    near_rows_hbm,
    near_cols_hbm,
    far_rows_hbm,
    far_slots_hbm,
    send_hbm,
    potentials,
    adjoint,
    charges,
    bases,
    couplings,
    near,
    near_rows,
    near_cols,
    far_rows,
    far_slots,
    send,
    idx_v,
    idx,
    bases32,
    bases_perm,
    coeffs,
    out_f,
    in_f,
    out_r,
    in_r,
    adj32,
    merged,
    place,
    fwd32,
    sums_f,
    sums_a,
    all_loads,
    part_out,
    part_in,
    in_sem,
    idx_sem,
    f_send,
    f_recv,
    r_send,
    r_recv,
    pair_send,
    pair_recv,
):
    cols = dims["col"]
    clusters, rank, block = bases.shape
    cap, peers = send.shape[1], send.shape[2]
    slots = peers * cap
    chunk = min(CHUNK, slots)
    chunks = slots // chunk
    group = block // rank
    tall = rank // group
    row, col, core = lax.axis_index("row"), lax.axis_index("col"), lax.axis_index("sub")
    me = row * cols + col
    other = 1 - core

    def peer_of(d):
        p = lax.rem(me + d, peers)
        return p, {"row": p // cols, "col": lax.rem(p, cols)}

    def fetch(src, dst, at):
        copy = pltpu.make_async_copy(src, dst, in_sem.at[at])
        copy.start()
        return copy

    get_rows = fetch(near_rows_hbm, near_rows, 0)
    get_cols = fetch(near_cols_hbm, near_cols, 1)
    get_bases = fetch(bases_hbm, bases, 2)
    get_loads = fetch(loads_hbm, all_loads.at[pl.ds(core * clusters, clusters)], 3)
    get_charges = fetch(charges_hbm, charges, 4)
    get_send = fetch(send_hbm, send, 5)
    get_far_rows = fetch(far_rows_hbm, far_rows, 6)
    get_far_slots = fetch(far_slots_hbm, far_slots, 7)
    get_couplings = fetch(couplings_hbm, couplings, 8)
    get_near = fetch(near_hbm, near, 9)

    barrier = pltpu.get_barrier_semaphore()
    pl.semaphore_signal(barrier, inc=1, device_id={"sub": other}, device_id_type=MESH)

    def greet(step):
        _, device = peer_of(step + 1)
        pl.semaphore_signal(barrier, inc=1, device_id=device, device_id_type=MESH)

    loop(peers - 1, greet)

    get_rows.wait()
    get_cols.wait()
    sorted_index(near_rows[...], near_cols[...], idx_v, 0)
    sorted_index(near_cols[...], near_rows[...], idx_v, 4)
    idx_copy = pltpu.make_async_copy(idx_v, idx, idx_sem)
    idx_copy.start()

    pl.semaphore_wait(barrier, peers)
    pair_loads = pltpu.make_async_remote_copy(
        src_ref=loads_hbm,
        dst_ref=all_loads.at[pl.ds(core * clusters, clusters)],
        send_sem=pair_send.at[0],
        recv_sem=pair_recv.at[0],
        device_id={"sub": other},
        device_id_type=MESH,
    )
    pair_loads.start()

    get_bases.wait()
    get_loads.wait()
    get_charges.wait()
    bases32[...] = bases[...].astype(f32).reshape(clusters * rank, block)
    for c in range(clusters):
        parts = [bases32[pl.ds(c * rank + i, tall, stride=group), :] for i in range(group)]
        bases_perm[c] = jnp.concatenate(parts, axis=0).astype(bf16)
        coeffs[c] = dot(bases[c], charges[c]).astype(bf16)
        adj32[pl.ds(c, rank, stride=clusters), :] = dot(bases_perm[c], all_loads[core * clusters + c])

    get_send.wait()

    def fill(p):
        for k in range(cap):
            out_f[p, k] = coeffs[jnp.maximum(send[0, k, p], 0)]

    loop(peers, fill)

    def far_copy(src, dst, send_sem, recv_sem, step):
        p, device = peer_of(step + 1)
        return pltpu.make_async_remote_copy(
            src_ref=src.at[p],
            dst_ref=dst.at[me],
            send_sem=send_sem.at[p],
            recv_sem=recv_sem.at[me],
            device_id=device,
            device_id_type=MESH,
        )

    def far_wait(src, dst, send_sem, recv_sem, step):
        p, device = peer_of(step + 1)
        return pltpu.make_async_remote_copy(
            src_ref=src.at[p],
            dst_ref=dst.at[p],
            send_sem=send_sem.at[p],
            recv_sem=recv_sem.at[p],
            device_id=device,
            device_id_type=MESH,
        )

    loop(peers - 1, lambda step: far_copy(out_f, in_f, f_send, f_recv, step).start())
    in_f[me] = out_f[me]

    get_far_rows.wait()
    get_far_slots.wait()
    get_couplings.wait()
    key = far_slots[...] * clusters + far_rows[...]
    pairs = key.shape[1]
    adj_flat = adj32[...].astype(bf16)
    span = chunk * rank

    def merge(ch):
        cells = lax.broadcasted_iota(jnp.int32, (chunk * clusters, pairs), 0) + ch * (
            chunk * clusters
        )
        hot = jnp.where(cells == key, 1.0, 0.0).astype(bf16)
        cell = dot(hot, couplings[...])
        for t in range(chunk):
            tile = jnp.concatenate(
                [
                    cell[t * clusters : (t + 1) * clusters, a * block : (a + 1) * block]
                    for a in range(tall)
                ],
                axis=0,
            )
            turned = tile.T.astype(bf16)
            for i in range(group):
                merged[ch, t * rank : (t + 1) * rank, i * block : (i + 1) * block] = turned[
                    i * rank : (i + 1) * rank
                ]
        back = dot(merged[ch], adj_flat).astype(bf16)
        per = chunk // cap
        out_r[pl.ds(ch * per, per)] = back.reshape(per, cap, rank, block)

    loop(chunks, merge)
    loop(peers - 1, lambda step: far_copy(out_r, in_r, r_send, r_recv, step).start())
    in_r[me] = out_r[me]

    idx_copy.wait()
    get_near.wait()
    segment_products(lambda b, t: dot(near[b], charges[t]), idx, 0, sums_f)
    for c in range(clusters):
        part_out[c] = sums_f[idx[3, other * clusters + c]].astype(bf16)
    pair_part = pltpu.make_async_remote_copy(
        src_ref=part_out,
        dst_ref=part_in,
        send_sem=pair_send.at[1],
        recv_sem=pair_recv.at[1],
        device_id={"sub": other},
        device_id_type=MESH,
    )
    pair_part.start()

    per = chunk // cap

    def placing(ch):
        lane = lax.broadcasted_iota(jnp.int32, (8, span), 1)
        target = jnp.full((8, span), -1, jnp.int32)
        for t in range(chunk):
            own = send[0, t % cap, ch * per + t // cap]
            target = jnp.where(lane // rank == t, own * rank + lane % rank, target)
        rows = lax.broadcasted_iota(jnp.int32, (clusters * rank, span), 0)
        place[ch] = jnp.where(rows == target[0:1], 1.0, 0.0).astype(bf16)

    loop(chunks, placing)

    loop(peers - 1, lambda step: far_wait(out_f, in_f, f_send, f_recv, step).wait_recv())
    fwd32[...] = jnp.zeros(fwd32.shape, f32)

    def forward(ch):
        arrived = in_f[pl.ds(ch * per, per)].reshape(span, block)
        fwd32[...] += dot_t(merged[ch], arrived)

    loop(chunks, forward)

    pltpu.make_async_remote_copy(
        src_ref=loads_hbm,
        dst_ref=all_loads.at[pl.ds(other * clusters, clusters)],
        send_sem=pair_send.at[0],
        recv_sem=pair_recv.at[0],
        device_id={"sub": other},
        device_id_type=MESH,
    ).wait_recv()
    segment_products(lambda b, s: dot_t(near[b], all_loads[s]), idx, 4, sums_a)

    loop(peers - 1, lambda step: far_wait(out_r, in_r, r_send, r_recv, step).wait_recv())
    far_adj = adj32
    far_adj[...] = jnp.zeros(far_adj.shape, f32)

    def scatter(ch):
        returned = in_r[pl.ds(ch * per, per)].reshape(span, block)
        far_adj[...] += dot(place[ch], returned)

    loop(chunks, scatter)
    for c in range(clusters):
        total = far_adj[c * rank : (c + 1) * rank]
        far = dot_t(bases[c], total.astype(bf16))
        adjoint[c] = (far + sums_a[idx[7, c]]).astype(bf16)

    pair_part.wait_recv()
    for c in range(clusters):
        far_c = fwd32[pl.ds(c, rank, stride=clusters), :].astype(bf16)
        far = dot_t(bases_perm[c], far_c)
        mine = sums_f[idx[3, core * clusters + c]]
        potentials[c] = (far + mine + part_in[c].astype(f32)).astype(bf16)

    pair_loads.wait_send()
    pair_part.wait_send()
    loop(peers - 1, lambda step: far_wait(out_f, in_f, f_send, f_recv, step).wait_send())
    loop(peers - 1, lambda step: far_wait(out_r, in_r, r_send, r_recv, step).wait_send())


def on_device(dims, *args):
    args = args[:-1] + (jnp.transpose(args[-1], (0, 2, 1)),)
    charges, loads, bases, couplings, near, near_rows, near_cols, far_rows, far_slots, send = args
    clusters, block, width = charges.shape
    rank = bases.shape[1]
    blocks = near.shape[0]
    cap, peers = send.shape[1], send.shape[2]
    chunk = min(CHUNK, peers * cap)
    vmem = pl.BlockSpec(memory_space=pltpu.VMEM)
    dma = pltpu.SemaphoreType.DMA
    slot_shape = (peers, cap, rank, width)
    full = jax.ShapeDtypeStruct((clusters, block, width), bf16)
    return pl.pallas_call(
        functools.partial(kernel, dims),
        out_shape=(full, full),
        in_specs=[pl.BlockSpec(memory_space=pl.ANY)] * 10,
        out_specs=(vmem, vmem),
        scratch_shapes=[
            pltpu.VMEM(charges.shape, bf16),
            pltpu.VMEM(bases.shape, bf16),
            pltpu.VMEM(couplings.shape, bf16),
            pltpu.VMEM(near.shape, bf16),
            pltpu.VMEM(near_rows.shape, jnp.int32),
            pltpu.VMEM(near_cols.shape, jnp.int32),
            pltpu.VMEM(far_rows.shape, jnp.int32),
            pltpu.VMEM(far_slots.shape, jnp.int32),
            pltpu.SMEM(send.shape, jnp.int32),
            pltpu.VMEM((8, 128), jnp.int32),
            pltpu.SMEM((8, 128), jnp.int32),
            pltpu.VMEM((clusters * rank, block), f32),
            pltpu.VMEM((clusters, rank, block), bf16),
            pltpu.VMEM((clusters, rank, width), bf16),
            pltpu.VMEM(slot_shape, bf16),
            pltpu.VMEM(slot_shape, bf16),
            pltpu.VMEM(slot_shape, bf16),
            pltpu.VMEM(slot_shape, bf16),
            pltpu.VMEM((clusters * rank, width), f32),
            pltpu.VMEM((peers * cap // chunk, chunk * rank, clusters * rank), bf16),
            pltpu.VMEM((peers * cap // chunk, clusters * rank, chunk * rank), bf16),
            pltpu.VMEM((clusters * rank, width), f32),
            pltpu.VMEM((blocks + 1, block, width), f32),
            pltpu.VMEM((blocks + 1, block, width), f32),
            pltpu.VMEM((2 * clusters, block, width), bf16),
            pltpu.VMEM((clusters, block, width), bf16),
            pltpu.VMEM((clusters, block, width), bf16),
            dma((10,)),
            dma,
            dma((peers,)),
            dma((peers,)),
            dma((peers,)),
            dma((peers,)),
            dma((2,)),
            dma((2,)),
        ],
        compiler_params=pltpu.CompilerParams(
            collective_id=0, has_side_effects=True, vmem_limit_bytes=62 * 1024 * 1024
        ),
        name="hierarchical",
    )(*args)


def solution(mesh):
    split = ("variant", "row", "col", "sub")
    owner = ("row", "col", "sub")
    in_specs = (
        P(split, None, None),
        P(split, None, None),
        P(split, None, None),
        P(split, None),
        P(split, None, None),
        P(owner, None),
        P(owner, None),
        P(owner, None),
        P(owner, None),
        P(owner, None, None),
    )
    out_specs = (P(split, None, None), P(split, None, None))
    return jax.shard_map(
        functools.partial(on_device, dict(mesh.shape)),
        mesh=mesh,
        in_specs=in_specs,
        out_specs=out_specs,
        check_vma=False,
    )
```

```python
import functools

import jax
import jax.numpy as jnp
from jax import lax
from jax.experimental import pallas as pl
from jax.experimental.pallas import tpu as pltpu
from jax.sharding import PartitionSpec as P

MESH = pl.DeviceIdType.MESH
f32 = jnp.float32
bf16 = jnp.bfloat16
UNROLL = 8
CHUNK = 16


def loop(count, body):
    if count <= 16:
        for step in range(count):
            body(step)
    else:

        def step_body(step, carry):
            body(step)
            return carry

        lax.fori_loop(0, count, step_body, 0)


def dot(a, b):
    return jnp.dot(a, b, preferred_element_type=f32)


def dot_t(a, b):
    return lax.dot_general(a, b, (((0,), (0,)), ((), ())), preferred_element_type=f32)


def sorted_index(keys_row, other_row, idx_ref, at):
    n = keys_row.shape[1]
    lane = lax.broadcasted_iota(jnp.int32, (n, n), 1)
    sub = lax.broadcasted_iota(jnp.int32, (n, n), 0)
    keys = jnp.broadcast_to(keys_row, (n, n))
    eye = lane == sub
    key_col = jnp.sum(jnp.where(eye, keys, 0), axis=1, keepdims=True)
    other_col = jnp.sum(
        jnp.where(eye, jnp.broadcast_to(other_row, (n, n)), 0), axis=1, keepdims=True
    )
    before = (keys < key_col) | ((keys == key_col) & (lane < sub))
    rank = jnp.sum(jnp.where(before, 1, 0), axis=1, keepdims=True)
    wide = (n, 128)
    lanes = lax.broadcasted_iota(jnp.int32, wide, 1)
    subs = lax.broadcasted_iota(jnp.int32, wide, 0)
    here = rank == lanes

    def pick(values):
        return jnp.sum(jnp.where(here, values, 0), axis=0, keepdims=True)

    idx_ref[at : at + 1, :] = pick(subs)
    idx_ref[at + 1 : at + 2, :] = pick(jnp.broadcast_to(key_col, wide))
    idx_ref[at + 2 : at + 3, :] = pick(jnp.broadcast_to(other_col, wide))
    upto = jnp.sum(jnp.where(key_col <= lanes, 1, 0), axis=0, keepdims=True)
    same = jnp.sum(jnp.where(key_col == lanes, 1, 0), axis=0, keepdims=True)
    idx_ref[at + 3 : at + 4, :] = jnp.where(same > 0, upto - 1, n)


def segment_products(product, idx, at, sums):
    n = sums.shape[0] - 1
    unroll = UNROLL if n % UNROLL == 0 else 1
    sums[n] = jnp.zeros(sums.shape[1:], f32)

    def body(step, total):
        terms = []
        for u in range(unroll):
            k = step * unroll + u
            terms.append(product(idx[at, k], idx[at + 2, k]))
        for u in range(unroll):
            k = step * unroll + u
            same = (idx[at + 1, k] == idx[at + 1, jnp.maximum(k - 1, 0)]) & (k > 0)
            total = total * jnp.where(same, 1.0, 0.0).astype(f32) + terms[u]
            sums[k] = total
        return total

    lax.fori_loop(0, n // unroll, body, jnp.zeros(sums.shape[1:], f32))


def kernel(
    dims,
    charges_hbm,
    loads_hbm,
    bases_hbm,
    couplings_hbm,
    near_hbm,
    near_rows_hbm,
    near_cols_hbm,
    far_rows_hbm,
    far_slots_hbm,
    send_hbm,
    potentials,
    adjoint,
    charges,
    bases,
    couplings,
    near,
    near_rows,
    near_cols,
    far_rows,
    far_slots,
    send,
    idx_v,
    idx,
    bases32,
    bases_perm,
    coeffs,
    out_f,
    in_f,
    out_r,
    in_r,
    adj32,
    merged,
    place,
    fwd32,
    sums_f,
    sums_a,
    all_loads,
    part_out,
    part_in,
    in_sem,
    idx_sem,
    f_send,
    f_recv,
    r_send,
    r_recv,
    pair_send,
    pair_recv,
):
    cols = dims["col"]
    clusters, rank, block = bases.shape
    cap, peers = send.shape[1], send.shape[2]
    slots = peers * cap
    chunk = min(CHUNK, slots)
    chunks = slots // chunk
    group = block // rank
    tall = rank // group
    row, col, core = lax.axis_index("row"), lax.axis_index("col"), lax.axis_index("sub")
    me = row * cols + col
    other = 1 - core

    def peer_of(d):
        if peers & (peers - 1):
            p = lax.rem(me + d, peers)
        else:
            p, bit = 0, 1
            while bit < peers:
                p = p + lax.rem(me // bit + (peers - d) // bit, 2) * bit
                bit *= 2
        return p, {"row": p // cols, "col": lax.rem(p, cols)}

    def fetch(src, dst, at):
        copy = pltpu.make_async_copy(src, dst, in_sem.at[at])
        copy.start()
        return copy

    get_bases = fetch(bases_hbm, bases, 0)
    get_charges = fetch(charges_hbm, charges, 1)
    get_send = fetch(send_hbm, send, 2)
    get_loads = fetch(loads_hbm, all_loads.at[pl.ds(core * clusters, clusters)], 3)
    get_couplings = fetch(couplings_hbm, couplings, 4)
    get_far_rows = fetch(far_rows_hbm, far_rows, 5)
    get_far_slots = fetch(far_slots_hbm, far_slots, 6)
    get_rows = fetch(near_rows_hbm, near_rows, 7)
    get_cols = fetch(near_cols_hbm, near_cols, 8)
    get_near = fetch(near_hbm, near, 9)

    barrier = pltpu.get_barrier_semaphore()
    pl.semaphore_signal(barrier, inc=1, device_id={"sub": other}, device_id_type=MESH)

    def greet(step):
        _, device = peer_of(step + 1)
        pl.semaphore_signal(barrier, inc=1, device_id=device, device_id_type=MESH)

    loop(peers - 1, greet)

    get_bases.wait()
    get_charges.wait()
    for c in range(clusters):
        coeffs[c] = dot(bases[c], charges[c]).astype(bf16)
    get_send.wait()

    def fill(p):
        for k in range(cap):
            out_f[p, k] = coeffs[jnp.maximum(send[0, k, p], 0)]

    loop(peers, fill)
    pl.semaphore_wait(barrier, peers)

    def far_copy(src, dst, send_sem, recv_sem, step):
        p, device = peer_of(step + 1)
        return pltpu.make_async_remote_copy(
            src_ref=src.at[p],
            dst_ref=dst.at[me],
            send_sem=send_sem.at[p],
            recv_sem=recv_sem.at[me],
            device_id=device,
            device_id_type=MESH,
        )

    def far_wait(src, dst, send_sem, recv_sem, step):
        p, device = peer_of(step + 1)
        return pltpu.make_async_remote_copy(
            src_ref=src.at[p],
            dst_ref=dst.at[p],
            send_sem=send_sem.at[p],
            recv_sem=recv_sem.at[p],
            device_id=device,
            device_id_type=MESH,
        )

    loop(peers - 1, lambda step: far_copy(out_f, in_f, f_send, f_recv, step).start())
    in_f[me] = out_f[me]
    pair_loads = pltpu.make_async_remote_copy(
        src_ref=loads_hbm,
        dst_ref=all_loads.at[pl.ds(core * clusters, clusters)],
        send_sem=pair_send.at[0],
        recv_sem=pair_recv.at[0],
        device_id={"sub": other},
        device_id_type=MESH,
    )
    pair_loads.start()

    get_loads.wait()
    bases32[...] = bases[...].astype(f32).reshape(clusters * rank, block)
    for c in range(clusters):
        parts = [bases32[pl.ds(c * rank + i, tall, stride=group), :] for i in range(group)]
        bases_perm[c] = jnp.concatenate(parts, axis=0).astype(bf16)
        adj32[pl.ds(c, rank, stride=clusters), :] = dot(
            bases_perm[c], all_loads[core * clusters + c]
        )

    get_far_rows.wait()
    get_far_slots.wait()
    get_couplings.wait()
    key = far_slots[...] * clusters + far_rows[...]
    pairs = key.shape[1]
    adj_flat = adj32[...].astype(bf16)
    span = chunk * rank

    def merge(ch):
        cells = lax.broadcasted_iota(jnp.int32, (chunk * clusters, pairs), 0) + ch * (
            chunk * clusters
        )
        hot = jnp.where(cells == key, 1.0, 0.0).astype(bf16)
        cell = dot(hot, couplings[...])
        for t in range(chunk):
            tile = jnp.concatenate(
                [
                    cell[t * clusters : (t + 1) * clusters, a * block : (a + 1) * block]
                    for a in range(tall)
                ],
                axis=0,
            )
            turned = tile.T.astype(bf16)
            for i in range(group):
                merged[ch, t * rank : (t + 1) * rank, i * block : (i + 1) * block] = turned[
                    i * rank : (i + 1) * rank
                ]
        back = dot(merged[ch], adj_flat).astype(bf16)
        per = chunk // cap
        out_r[pl.ds(ch * per, per)] = back.reshape(per, cap, rank, block)

    loop(chunks, merge)
    loop(peers - 1, lambda step: far_copy(out_r, in_r, r_send, r_recv, step).start())
    in_r[me] = out_r[me]

    get_rows.wait()
    get_cols.wait()
    sorted_index(near_rows[...], near_cols[...], idx_v, 0)
    sorted_index(near_cols[...], near_rows[...], idx_v, 4)
    idx_copy = pltpu.make_async_copy(idx_v, idx, idx_sem)
    idx_copy.start()

    idx_copy.wait()
    get_near.wait()
    segment_products(lambda b, t: dot(near[b], charges[t]), idx, 0, sums_f)
    for c in range(clusters):
        part_out[c] = sums_f[idx[3, other * clusters + c]].astype(bf16)
    pair_part = pltpu.make_async_remote_copy(
        src_ref=part_out,
        dst_ref=part_in,
        send_sem=pair_send.at[1],
        recv_sem=pair_recv.at[1],
        device_id={"sub": other},
        device_id_type=MESH,
    )
    pair_part.start()

    per = chunk // cap

    def placing(ch):
        lane = lax.broadcasted_iota(jnp.int32, (8, span), 1)
        target = jnp.full((8, span), -1, jnp.int32)
        for t in range(chunk):
            own = send[0, t % cap, ch * per + t // cap]
            target = jnp.where(lane // rank == t, own * rank + lane % rank, target)
        rows = lax.broadcasted_iota(jnp.int32, (clusters * rank, span), 0)
        place[ch] = jnp.where(rows == target[0:1], 1.0, 0.0).astype(bf16)

    loop(chunks, placing)

    loop(peers - 1, lambda step: far_wait(out_f, in_f, f_send, f_recv, step).wait_recv())
    fwd32[...] = jnp.zeros(fwd32.shape, f32)

    def forward(ch):
        arrived = in_f[pl.ds(ch * per, per)].reshape(span, block)
        fwd32[...] += dot_t(merged[ch], arrived)

    loop(chunks, forward)

    pltpu.make_async_remote_copy(
        src_ref=loads_hbm,
        dst_ref=all_loads.at[pl.ds(other * clusters, clusters)],
        send_sem=pair_send.at[0],
        recv_sem=pair_recv.at[0],
        device_id={"sub": other},
        device_id_type=MESH,
    ).wait_recv()
    segment_products(lambda b, s: dot_t(near[b], all_loads[s]), idx, 4, sums_a)

    loop(peers - 1, lambda step: far_wait(out_r, in_r, r_send, r_recv, step).wait_recv())
    far_adj = adj32
    far_adj[...] = jnp.zeros(far_adj.shape, f32)

    def scatter(ch):
        returned = in_r[pl.ds(ch * per, per)].reshape(span, block)
        far_adj[...] += dot(place[ch], returned)

    loop(chunks, scatter)
    for c in range(clusters):
        total = far_adj[c * rank : (c + 1) * rank]
        far = dot_t(bases[c], total.astype(bf16))
        adjoint[c] = (far + sums_a[idx[7, c]]).astype(bf16)

    pair_part.wait_recv()
    for c in range(clusters):
        far_c = fwd32[pl.ds(c, rank, stride=clusters), :].astype(bf16)
        far = dot_t(bases_perm[c], far_c)
        mine = sums_f[idx[3, core * clusters + c]]
        potentials[c] = (far + mine + part_in[c].astype(f32)).astype(bf16)

    pair_loads.wait_send()
    pair_part.wait_send()
    loop(peers - 1, lambda step: far_wait(out_f, in_f, f_send, f_recv, step).wait_send())
    loop(peers - 1, lambda step: far_wait(out_r, in_r, r_send, r_recv, step).wait_send())


def write_out(potentials, adjoint, potentials_hbm, adjoint_hbm, sem):
    first = pltpu.make_async_copy(potentials, potentials_hbm, sem.at[0])
    second = pltpu.make_async_copy(adjoint, adjoint_hbm, sem.at[1])
    first.start()
    second.start()
    first.wait()
    second.wait()


def on_device(dims, *args):
    args = args[:-1] + (jnp.transpose(args[-1], (0, 2, 1)),)
    charges, loads, bases, couplings, near, near_rows, near_cols, far_rows, far_slots, send = args
    clusters, block, width = charges.shape
    rank = bases.shape[1]
    blocks = near.shape[0]
    cap, peers = send.shape[1], send.shape[2]
    chunk = min(CHUNK, peers * cap)
    vmem = pl.BlockSpec(memory_space=pltpu.VMEM)
    dma = pltpu.SemaphoreType.DMA
    slot_shape = (peers, cap, rank, width)
    full = jax.ShapeDtypeStruct((clusters, block, width), bf16)
    results = pl.pallas_call(
        functools.partial(kernel, dims),
        out_shape=(pltpu.VMEM(full.shape, bf16),) * 2,
        in_specs=[pl.BlockSpec(memory_space=pltpu.HBM)] * 10,
        out_specs=(vmem, vmem),
        scratch_shapes=[
            pltpu.VMEM(charges.shape, bf16),
            pltpu.VMEM(bases.shape, bf16),
            pltpu.VMEM(couplings.shape, bf16),
            pltpu.VMEM(near.shape, bf16),
            pltpu.VMEM(near_rows.shape, jnp.int32),
            pltpu.VMEM(near_cols.shape, jnp.int32),
            pltpu.VMEM(far_rows.shape, jnp.int32),
            pltpu.VMEM(far_slots.shape, jnp.int32),
            pltpu.SMEM(send.shape, jnp.int32),
            pltpu.VMEM((8, 128), jnp.int32),
            pltpu.SMEM((8, 128), jnp.int32),
            pltpu.VMEM((clusters * rank, block), f32),
            pltpu.VMEM((clusters, rank, block), bf16),
            pltpu.VMEM((clusters, rank, width), bf16),
            pltpu.VMEM(slot_shape, bf16),
            pltpu.VMEM(slot_shape, bf16),
            pltpu.VMEM(slot_shape, bf16),
            pltpu.VMEM(slot_shape, bf16),
            pltpu.VMEM((clusters * rank, width), f32),
            pltpu.VMEM((peers * cap // chunk, chunk * rank, clusters * rank), bf16),
            pltpu.VMEM((peers * cap // chunk, clusters * rank, chunk * rank), bf16),
            pltpu.VMEM((clusters * rank, width), f32),
            pltpu.VMEM((blocks + 1, block, width), f32),
            pltpu.VMEM((blocks + 1, block, width), f32),
            pltpu.VMEM((2 * clusters, block, width), bf16),
            pltpu.VMEM((clusters, block, width), bf16),
            pltpu.VMEM((clusters, block, width), bf16),
            dma((10,)),
            dma,
            dma((peers,)),
            dma((peers,)),
            dma((peers,)),
            dma((peers,)),
            dma((2,)),
            dma((2,)),
        ],
        compiler_params=pltpu.CompilerParams(
            collective_id=0, has_side_effects=True, vmem_limit_bytes=54 * 1024 * 1024
        ),
        name="hierarchical",
    )(*args)
    return pl.pallas_call(
        write_out,
        out_shape=(full, full),
        in_specs=[vmem] * 2,
        out_specs=(pl.BlockSpec(memory_space=pltpu.HBM),) * 2,
        scratch_shapes=[dma((2,))],
        name="write_out",
    )(*results)


def solution(mesh):
    split = ("variant", "row", "col", "sub")
    owner = ("row", "col", "sub")
    in_specs = (
        P(split, None, None),
        P(split, None, None),
        P(split, None, None),
        P(split, None),
        P(split, None, None),
        P(owner, None),
        P(owner, None),
        P(owner, None),
        P(owner, None),
        P(owner, None, None),
    )
    out_specs = (P(split, None, None), P(split, None, None))
    return jax.shard_map(
        functools.partial(on_device, dict(mesh.shape)),
        mesh=mesh,
        in_specs=in_specs,
        out_specs=out_specs,
        check_vma=False,
    )
```

```python
import functools

import jax
import jax.numpy as jnp
from jax import lax
from jax.experimental import pallas as pl
from jax.experimental.pallas import tpu as pltpu
from jax.sharding import PartitionSpec as P

MESH = pl.DeviceIdType.MESH
f32 = jnp.float32
bf16 = jnp.bfloat16
UNROLL = 8
CHUNK = 16
PIECES = 4


def loop(count, body):
    if count <= 16:
        for step in range(count):
            body(step)
    else:

        def step_body(step, carry):
            body(step)
            return carry

        lax.fori_loop(0, count, step_body, 0)


def dot(a, b):
    return jnp.dot(a, b, preferred_element_type=f32)


def dot_t(a, b):
    return lax.dot_general(a, b, (((0,), (0,)), ((), ())), preferred_element_type=f32)


def sorted_index(keys_row, other_row, idx_ref, at):
    n = keys_row.shape[1]
    lane = lax.broadcasted_iota(jnp.int32, (n, n), 1)
    sub = lax.broadcasted_iota(jnp.int32, (n, n), 0)
    keys = jnp.broadcast_to(keys_row, (n, n))
    eye = lane == sub
    key_col = jnp.sum(jnp.where(eye, keys, 0), axis=1, keepdims=True)
    other_col = jnp.sum(
        jnp.where(eye, jnp.broadcast_to(other_row, (n, n)), 0), axis=1, keepdims=True
    )
    before = (keys < key_col) | ((keys == key_col) & (lane < sub))
    rank = jnp.sum(jnp.where(before, 1, 0), axis=1, keepdims=True)
    wide = (n, 128)
    lanes = lax.broadcasted_iota(jnp.int32, wide, 1)
    subs = lax.broadcasted_iota(jnp.int32, wide, 0)
    here = rank == lanes

    def pick(values):
        return jnp.sum(jnp.where(here, values, 0), axis=0, keepdims=True)

    idx_ref[at : at + 1, :] = pick(subs)
    idx_ref[at + 1 : at + 2, :] = pick(jnp.broadcast_to(key_col, wide))
    idx_ref[at + 2 : at + 3, :] = pick(jnp.broadcast_to(other_col, wide))
    upto = jnp.sum(jnp.where(key_col <= lanes, 1, 0), axis=0, keepdims=True)
    same = jnp.sum(jnp.where(key_col == lanes, 1, 0), axis=0, keepdims=True)
    idx_ref[at + 3 : at + 4, :] = jnp.where(same > 0, upto - 1, n)


def segment_products(product, idx, at, sums):
    n = sums.shape[0] - 1
    unroll = UNROLL if n % UNROLL == 0 else 1
    sums[n] = jnp.zeros(sums.shape[1:], f32)

    def body(step, total):
        terms = []
        for u in range(unroll):
            k = step * unroll + u
            terms.append(product(idx[at, k], idx[at + 2, k]))
        for u in range(unroll):
            k = step * unroll + u
            same = (idx[at + 1, k] == idx[at + 1, jnp.maximum(k - 1, 0)]) & (k > 0)
            total = total * jnp.where(same, 1.0, 0.0).astype(f32) + terms[u]
            sums[k] = total
        return total

    lax.fori_loop(0, n // unroll, body, jnp.zeros(sums.shape[1:], f32))


def kernel(
    dims,
    charges_hbm,
    loads_hbm,
    bases_hbm,
    couplings_hbm,
    near_hbm,
    near_rows_hbm,
    near_cols_hbm,
    far_rows_hbm,
    far_slots_hbm,
    send_hbm,
    potentials,
    near_adj,
    far_adj,
    bases,
    charges,
    couplings,
    near,
    near_rows,
    near_cols,
    far_rows,
    far_slots,
    send,
    idx_v,
    idx,
    bases32,
    bases_perm,
    coeffs,
    out_f,
    in_f,
    out_r,
    in_r,
    adj32,
    merged,
    place,
    fwd32,
    sums_f,
    sums_a,
    all_loads,
    part_out,
    part_in,
    in_sem,
    idx_sem,
    f_send,
    f_recv,
    r_send,
    r_recv,
    pair_send,
    pair_recv,
):
    cols = dims["col"]
    clusters, rank, block = bases.shape
    cap, peers = send.shape[1], send.shape[2]
    slots = peers * cap
    chunk = min(CHUNK, slots)
    chunks = slots // chunk
    group = block // rank
    tall = rank // group
    row, col, core = lax.axis_index("row"), lax.axis_index("col"), lax.axis_index("sub")
    me = row * cols + col
    other = 1 - core

    def peer_of(d):
        if peers & (peers - 1):
            p = lax.rem(me + d, peers)
        else:
            p, bit = 0, 1
            while bit < peers:
                p = p + lax.rem(me // bit + (peers - d) // bit, 2) * bit
                bit *= 2
        return p, {"row": p // cols, "col": lax.rem(p, cols)}

    def fetch(src, dst, at):
        copy = pltpu.make_async_copy(src, dst, in_sem.at[at])
        copy.start()
        return copy

    def fetch_pieces(src, dst, at):
        size = src.shape[0] // PIECES
        return [
            fetch(src.at[pl.ds(i * size, size)], dst.at[pl.ds(i * size, size)], at + i)
            for i in range(PIECES)
        ]

    get_bases = fetch(bases_hbm, bases, 0)
    get_charges = fetch_pieces(charges_hbm, charges, 10)
    get_send = fetch(send_hbm, send, 2)
    get_loads = fetch(loads_hbm, all_loads.at[pl.ds(core * clusters, clusters)], 3)
    get_couplings = fetch(couplings_hbm, couplings, 4)
    get_far_rows = fetch(far_rows_hbm, far_rows, 5)
    get_far_slots = fetch(far_slots_hbm, far_slots, 6)
    get_rows = fetch(near_rows_hbm, near_rows, 7)
    get_cols = fetch(near_cols_hbm, near_cols, 8)
    get_near = fetch_pieces(near_hbm, near, 10 + PIECES)

    barrier = pltpu.get_barrier_semaphore()
    pl.semaphore_signal(barrier, inc=1, device_id={"sub": other}, device_id_type=MESH)

    def greet(step):
        _, device = peer_of(step + 1)
        pl.semaphore_signal(barrier, inc=1, device_id=device, device_id_type=MESH)

    loop(peers - 1, greet)

    get_bases.wait()
    for c in range(clusters):
        if c % (clusters // PIECES) == 0:
            get_charges[c // (clusters // PIECES)].wait()
        coeffs[c] = dot(bases[c], charges[c]).astype(bf16)
    get_send.wait()

    def fill(p):
        for k in range(cap):
            out_f[p, k] = coeffs[jnp.maximum(send[0, k, p], 0)]

    loop(peers, fill)
    pl.semaphore_wait(barrier, peers)

    def far_copy(src, dst, send_sem, recv_sem, step):
        p, device = peer_of(step + 1)
        return pltpu.make_async_remote_copy(
            src_ref=src.at[p],
            dst_ref=dst.at[me],
            send_sem=send_sem.at[p],
            recv_sem=recv_sem.at[me],
            device_id=device,
            device_id_type=MESH,
        )

    def far_wait(src, dst, send_sem, recv_sem, step):
        p, device = peer_of(step + 1)
        return pltpu.make_async_remote_copy(
            src_ref=src.at[p],
            dst_ref=dst.at[p],
            send_sem=send_sem.at[p],
            recv_sem=recv_sem.at[p],
            device_id=device,
            device_id_type=MESH,
        )

    loop(peers - 1, lambda step: far_copy(out_f, in_f, f_send, f_recv, step).start())
    in_f[me] = out_f[me]
    pair_loads = pltpu.make_async_remote_copy(
        src_ref=loads_hbm,
        dst_ref=all_loads.at[pl.ds(core * clusters, clusters)],
        send_sem=pair_send.at[0],
        recv_sem=pair_recv.at[0],
        device_id={"sub": other},
        device_id_type=MESH,
    )
    pair_loads.start()

    get_loads.wait()
    bases32[...] = bases[...].astype(f32).reshape(clusters * rank, block)
    for c in range(clusters):
        parts = [bases32[pl.ds(c * rank + i, tall, stride=group), :] for i in range(group)]
        bases_perm[c] = jnp.concatenate(parts, axis=0).astype(bf16)
        adj32[pl.ds(c, rank, stride=clusters), :] = dot(
            bases_perm[c], all_loads[core * clusters + c]
        )

    get_far_rows.wait()
    get_far_slots.wait()
    get_couplings.wait()
    key = far_slots[...] * clusters + far_rows[...]
    pairs = key.shape[1]
    adj_flat = adj32[...].astype(bf16)
    span = chunk * rank

    def merge(ch):
        cells = lax.broadcasted_iota(jnp.int32, (chunk * clusters, pairs), 0) + ch * (
            chunk * clusters
        )
        hot = jnp.where(cells == key, 1.0, 0.0).astype(bf16)
        cell = dot(hot, couplings[...])
        for t in range(chunk):
            tile = jnp.concatenate(
                [
                    cell[t * clusters : (t + 1) * clusters, a * block : (a + 1) * block]
                    for a in range(tall)
                ],
                axis=0,
            )
            turned = tile.T.astype(bf16)
            for i in range(group):
                merged[ch, t * rank : (t + 1) * rank, i * block : (i + 1) * block] = turned[
                    i * rank : (i + 1) * rank
                ]
        back = dot(merged[ch], adj_flat).astype(bf16)
        per = chunk // cap
        out_r[pl.ds(ch * per, per)] = back.reshape(per, cap, rank, block)

    loop(chunks, merge)
    loop(peers - 1, lambda step: far_copy(out_r, in_r, r_send, r_recv, step).start())
    in_r[me] = out_r[me]

    get_rows.wait()
    get_cols.wait()
    sorted_index(near_rows[...], near_cols[...], idx_v, 0)
    sorted_index(near_cols[...], near_rows[...], idx_v, 4)
    idx_copy = pltpu.make_async_copy(idx_v, idx, idx_sem)
    idx_copy.start()

    idx_copy.wait()
    for piece in get_near:
        piece.wait()
    segment_products(lambda b, t: dot(near[b], charges[t]), idx, 0, sums_f)
    for c in range(clusters):
        part_out[c] = sums_f[idx[3, other * clusters + c]].astype(bf16)
    pair_part = pltpu.make_async_remote_copy(
        src_ref=part_out,
        dst_ref=part_in,
        send_sem=pair_send.at[1],
        recv_sem=pair_recv.at[1],
        device_id={"sub": other},
        device_id_type=MESH,
    )
    pair_part.start()

    per = chunk // cap

    def placing(ch):
        lane = lax.broadcasted_iota(jnp.int32, (8, span), 1)
        target = jnp.full((8, span), -1, jnp.int32)
        for t in range(chunk):
            own = send[0, t % cap, ch * per + t // cap]
            target = jnp.where(lane // rank == t, own * rank + lane % rank, target)
        rows = lax.broadcasted_iota(jnp.int32, (clusters * rank, span), 0)
        place[ch] = jnp.where(rows == target[0:1], 1.0, 0.0).astype(bf16)

    loop(chunks, placing)

    loop(peers - 1, lambda step: far_wait(out_f, in_f, f_send, f_recv, step).wait_recv())
    fwd32[...] = jnp.zeros(fwd32.shape, f32)

    def forward(ch):
        arrived = in_f[pl.ds(ch * per, per)].reshape(span, block)
        fwd32[...] += dot_t(merged[ch], arrived)

    loop(chunks, forward)

    pltpu.make_async_remote_copy(
        src_ref=loads_hbm,
        dst_ref=all_loads.at[pl.ds(other * clusters, clusters)],
        send_sem=pair_send.at[0],
        recv_sem=pair_recv.at[0],
        device_id={"sub": other},
        device_id_type=MESH,
    ).wait_recv()
    segment_products(lambda b, s: dot_t(near[b], all_loads[s]), idx, 4, sums_a)

    for c in range(clusters):
        near_adj[c] = sums_a[idx[7, c]]
    pair_part.wait_recv()
    for c in range(clusters):
        far_c = fwd32[pl.ds(c, rank, stride=clusters), :].astype(bf16)
        far = dot_t(bases_perm[c], far_c)
        mine = sums_f[idx[3, core * clusters + c]]
        potentials[c] = (far + mine + part_in[c].astype(f32)).astype(bf16)

    loop(peers - 1, lambda step: far_wait(out_r, in_r, r_send, r_recv, step).wait_recv())
    total = jnp.zeros(adj32.shape, f32)
    if chunks == 1:
        total = dot(place[0], in_r[...].reshape(span, block))
    else:
        adj32[...] = total

        def scatter(ch):
            returned = in_r[pl.ds(ch * per, per)].reshape(span, block)
            adj32[...] += dot(place[ch], returned)

        loop(chunks, scatter)
        total = adj32[...]
    far_adj[...] = total.astype(bf16).reshape(clusters, rank, block)

    pair_loads.wait_send()
    pair_part.wait_send()
    loop(peers - 1, lambda step: far_wait(out_f, in_f, f_send, f_recv, step).wait_send())
    loop(peers - 1, lambda step: far_wait(out_r, in_r, r_send, r_recv, step).wait_send())


def finish(potentials, near_adj, far_adj, bases, potentials_hbm, adjoint_hbm, adjoint, sem):
    clusters = potentials.shape[0]
    size = clusters // PIECES
    copies = []

    def write(src, dst, piece, at):
        part = pl.ds(piece * size, size)
        copies.append(pltpu.make_async_copy(src.at[part], dst.at[part], sem.at[at]))
        copies[-1].start()

    for piece in range(PIECES):
        write(potentials, potentials_hbm, piece, piece)
    for piece in range(PIECES):
        for c in range(piece * size, (piece + 1) * size):
            adjoint[c] = (dot_t(bases[c], far_adj[c]) + near_adj[c]).astype(bf16)
        write(adjoint, adjoint_hbm, piece, PIECES + piece)
    for copy in copies:
        copy.wait()


def on_device(dims, *args):
    args = args[:-1] + (jnp.transpose(args[-1], (0, 2, 1)),)
    charges, loads, bases, couplings, near, near_rows, near_cols, far_rows, far_slots, send = args
    clusters, block, width = charges.shape
    rank = bases.shape[1]
    blocks = near.shape[0]
    cap, peers = send.shape[1], send.shape[2]
    chunk = min(CHUNK, peers * cap)
    vmem = pl.BlockSpec(memory_space=pltpu.VMEM)
    dma = pltpu.SemaphoreType.DMA
    slot_shape = (peers, cap, rank, width)
    full = jax.ShapeDtypeStruct((clusters, block, width), bf16)
    results = pl.pallas_call(
        functools.partial(kernel, dims),
        out_shape=(
            pltpu.VMEM(full.shape, bf16),
            pltpu.VMEM(full.shape, f32),
            pltpu.VMEM((clusters, rank, width), bf16),
            pltpu.VMEM(bases.shape, bf16),
        ),
        in_specs=[pl.BlockSpec(memory_space=pltpu.HBM)] * 10,
        out_specs=(vmem,) * 4,
        scratch_shapes=[
            pltpu.VMEM(charges.shape, bf16),
            pltpu.VMEM(couplings.shape, bf16),
            pltpu.VMEM(near.shape, bf16),
            pltpu.VMEM(near_rows.shape, jnp.int32),
            pltpu.VMEM(near_cols.shape, jnp.int32),
            pltpu.VMEM(far_rows.shape, jnp.int32),
            pltpu.VMEM(far_slots.shape, jnp.int32),
            pltpu.SMEM(send.shape, jnp.int32),
            pltpu.VMEM((8, 128), jnp.int32),
            pltpu.SMEM((8, 128), jnp.int32),
            pltpu.VMEM((clusters * rank, block), f32),
            pltpu.VMEM((clusters, rank, block), bf16),
            pltpu.VMEM((clusters, rank, width), bf16),
            pltpu.VMEM(slot_shape, bf16),
            pltpu.VMEM(slot_shape, bf16),
            pltpu.VMEM(slot_shape, bf16),
            pltpu.VMEM(slot_shape, bf16),
            pltpu.VMEM((clusters * rank, width), f32),
            pltpu.VMEM((peers * cap // chunk, chunk * rank, clusters * rank), bf16),
            pltpu.VMEM((peers * cap // chunk, clusters * rank, chunk * rank), bf16),
            pltpu.VMEM((clusters * rank, width), f32),
            pltpu.VMEM((blocks + 1, block, width), f32),
            pltpu.VMEM((blocks + 1, block, width), f32),
            pltpu.VMEM((2 * clusters, block, width), bf16),
            pltpu.VMEM((clusters, block, width), bf16),
            pltpu.VMEM((clusters, block, width), bf16),
            dma((10 + 2 * PIECES,)),
            dma,
            dma((peers,)),
            dma((peers,)),
            dma((peers,)),
            dma((peers,)),
            dma((2,)),
            dma((2,)),
        ],
        compiler_params=pltpu.CompilerParams(
            collective_id=0, has_side_effects=True, vmem_limit_bytes=54 * 1024 * 1024
        ),
        name="hierarchical",
    )(*args)
    return pl.pallas_call(
        finish,
        out_shape=(full, full),
        in_specs=[vmem] * 4,
        out_specs=(pl.BlockSpec(memory_space=pltpu.HBM),) * 2,
        scratch_shapes=[pltpu.VMEM(full.shape, bf16), dma((2 * PIECES,))],
        compiler_params=pltpu.CompilerParams(vmem_limit_bytes=4 * 1024 * 1024),
        name="finish",
    )(*results)


def solution(mesh):
    split = ("variant", "row", "col", "sub")
    owner = ("row", "col", "sub")
    in_specs = (
        P(split, None, None),
        P(split, None, None),
        P(split, None, None),
        P(split, None),
        P(split, None, None),
        P(owner, None),
        P(owner, None),
        P(owner, None),
        P(owner, None),
        P(owner, None, None),
    )
    out_specs = (P(split, None, None), P(split, None, None))
    return jax.shard_map(
        functools.partial(on_device, dict(mesh.shape)),
        mesh=mesh,
        in_specs=in_specs,
        out_specs=out_specs,
        check_vma=False,
    )
```

```python
import functools

import jax
import jax.numpy as jnp
from jax import lax
from jax.experimental import pallas as pl
from jax.experimental.pallas import tpu as pltpu
from jax.sharding import PartitionSpec as P

MESH = pl.DeviceIdType.MESH
f32 = jnp.float32
bf16 = jnp.bfloat16
UNROLL = 8
CHUNK = 16
PIECES = 4


def loop(count, body):
    if count <= 16:
        for step in range(count):
            body(step)
    else:

        def step_body(step, carry):
            body(step)
            return carry

        lax.fori_loop(0, count, step_body, 0)


def dot(a, b):
    return jnp.dot(a, b, preferred_element_type=f32)


def dot_t(a, b):
    return lax.dot_general(a, b, (((0,), (0,)), ((), ())), preferred_element_type=f32)


def sorted_index(keys_row, other_row, idx_ref, at):
    n = keys_row.shape[1]
    lane = lax.broadcasted_iota(jnp.int32, (n, n), 1)
    sub = lax.broadcasted_iota(jnp.int32, (n, n), 0)
    keys = jnp.broadcast_to(keys_row, (n, n))
    eye = lane == sub
    key_col = jnp.sum(jnp.where(eye, keys, 0), axis=1, keepdims=True)
    other_col = jnp.sum(
        jnp.where(eye, jnp.broadcast_to(other_row, (n, n)), 0), axis=1, keepdims=True
    )
    before = (keys < key_col) | ((keys == key_col) & (lane < sub))
    rank = jnp.sum(jnp.where(before, 1, 0), axis=1, keepdims=True)
    wide = (n, 128)
    lanes = lax.broadcasted_iota(jnp.int32, wide, 1)
    subs = lax.broadcasted_iota(jnp.int32, wide, 0)
    here = rank == lanes

    def pick(values):
        return jnp.sum(jnp.where(here, values, 0), axis=0, keepdims=True)

    idx_ref[at : at + 1, :] = pick(subs)
    idx_ref[at + 1 : at + 2, :] = pick(jnp.broadcast_to(key_col, wide))
    idx_ref[at + 2 : at + 3, :] = pick(jnp.broadcast_to(other_col, wide))
    upto = jnp.sum(jnp.where(key_col <= lanes, 1, 0), axis=0, keepdims=True)
    same = jnp.sum(jnp.where(key_col == lanes, 1, 0), axis=0, keepdims=True)
    idx_ref[at + 3 : at + 4, :] = jnp.where(same > 0, upto - 1, n)


def segment_products(product, idx, at, sums):
    n = sums.shape[0] - 1
    unroll = UNROLL if n % UNROLL == 0 else 1
    sums[n] = jnp.zeros(sums.shape[1:], f32)

    def body(step, total):
        terms = []
        for u in range(unroll):
            k = step * unroll + u
            terms.append(product(idx[at, k], idx[at + 2, k]))
        for u in range(unroll):
            k = step * unroll + u
            same = (idx[at + 1, k] == idx[at + 1, jnp.maximum(k - 1, 0)]) & (k > 0)
            total = total * jnp.where(same, 1.0, 0.0).astype(f32) + terms[u]
            sums[k] = total
        return total

    lax.fori_loop(0, n // unroll, body, jnp.zeros(sums.shape[1:], f32))


def kernel(
    dims,
    charges_hbm,
    loads_hbm,
    bases_hbm,
    couplings_hbm,
    near_hbm,
    near_rows_hbm,
    near_cols_hbm,
    far_rows_hbm,
    far_slots_hbm,
    send_hbm,
    potentials,
    near_adj,
    far_adj,
    bases,
    charges,
    couplings,
    near,
    near_rows,
    near_cols,
    far_rows,
    far_slots,
    send,
    idx_v,
    idx,
    bases32,
    bases_perm,
    coeffs,
    out_f,
    in_f,
    out_r,
    in_r,
    adj32,
    merged,
    place,
    fwd32,
    sums_f,
    sums_a,
    all_loads,
    part_out,
    part_in,
    in_sem,
    idx_sem,
    f_send,
    f_recv,
    r_send,
    r_recv,
    pair_send,
    pair_recv,
):
    cols = dims["col"]
    clusters, rank, block = bases.shape
    cap, peers = send.shape[1], send.shape[2]
    slots = peers * cap
    chunk = min(CHUNK, slots)
    chunks = slots // chunk
    group = block // rank
    tall = rank // group
    row, col, core = lax.axis_index("row"), lax.axis_index("col"), lax.axis_index("sub")
    me = row * cols + col
    other = 1 - core

    def peer_of(d):
        if peers & (peers - 1):
            p = lax.rem(me + d, peers)
        else:
            p, bit = 0, 1
            while bit < peers:
                p = p + lax.rem(me // bit + (peers - d) // bit, 2) * bit
                bit *= 2
        return p, {"row": p // cols, "col": lax.rem(p, cols)}

    barrier = pltpu.get_barrier_semaphore()
    pl.semaphore_signal(barrier, inc=1, device_id={"sub": other}, device_id_type=MESH)

    def greet(step):
        _, device = peer_of(step + 1)
        pl.semaphore_signal(barrier, inc=1, device_id=device, device_id_type=MESH)

    loop(peers - 1, greet)

    def fetch(src, dst, at):
        copy = pltpu.make_async_copy(src, dst, in_sem.at[at])
        copy.start()
        return copy

    def fetch_pieces(src, dst, at):
        size = src.shape[0] // PIECES
        return [
            fetch(src.at[pl.ds(i * size, size)], dst.at[pl.ds(i * size, size)], at + i)
            for i in range(PIECES)
        ]

    get_bases = fetch(bases_hbm, bases, 0)
    get_charges = fetch_pieces(charges_hbm, charges, 10)
    get_send = fetch(send_hbm, send, 2)
    get_loads = fetch(loads_hbm, all_loads.at[pl.ds(core * clusters, clusters)], 3)
    get_couplings = fetch(couplings_hbm, couplings, 4)
    get_far_rows = fetch(far_rows_hbm, far_rows, 5)
    get_far_slots = fetch(far_slots_hbm, far_slots, 6)
    get_rows = fetch(near_rows_hbm, near_rows, 7)
    get_cols = fetch(near_cols_hbm, near_cols, 8)
    get_near = fetch_pieces(near_hbm, near, 10 + PIECES)

    get_bases.wait()
    for c in range(clusters):
        if c % (clusters // PIECES) == 0:
            get_charges[c // (clusters // PIECES)].wait()
        coeffs[c] = dot(bases[c], charges[c]).astype(bf16)
    get_send.wait()

    def fill(p):
        for k in range(cap):
            out_f[p, k] = coeffs[jnp.maximum(send[0, k, p], 0)]

    loop(peers, fill)
    pl.semaphore_wait(barrier, peers)

    def far_copy(src, dst, send_sem, recv_sem, step):
        p, device = peer_of(step + 1)
        return pltpu.make_async_remote_copy(
            src_ref=src.at[p],
            dst_ref=dst.at[me],
            send_sem=send_sem.at[p],
            recv_sem=recv_sem.at[me],
            device_id=device,
            device_id_type=MESH,
        )

    def far_wait(src, dst, send_sem, recv_sem, step):
        p, device = peer_of(step + 1)
        return pltpu.make_async_remote_copy(
            src_ref=src.at[p],
            dst_ref=dst.at[p],
            send_sem=send_sem.at[p],
            recv_sem=recv_sem.at[p],
            device_id=device,
            device_id_type=MESH,
        )

    loop(peers - 1, lambda step: far_copy(out_f, in_f, f_send, f_recv, step).start())
    in_f[me] = out_f[me]
    pair_loads = pltpu.make_async_remote_copy(
        src_ref=loads_hbm,
        dst_ref=all_loads.at[pl.ds(core * clusters, clusters)],
        send_sem=pair_send.at[0],
        recv_sem=pair_recv.at[0],
        device_id={"sub": other},
        device_id_type=MESH,
    )
    pair_loads.start()

    get_loads.wait()
    bases32[...] = bases[...].astype(f32).reshape(clusters * rank, block)
    for c in range(clusters):
        parts = [bases32[pl.ds(c * rank + i, tall, stride=group), :] for i in range(group)]
        bases_perm[c] = jnp.concatenate(parts, axis=0).astype(bf16)
        adj32[pl.ds(c, rank, stride=clusters), :] = dot(
            bases_perm[c], all_loads[core * clusters + c]
        )

    get_far_rows.wait()
    get_far_slots.wait()
    get_couplings.wait()
    key = far_slots[...] * clusters + far_rows[...]
    pairs = key.shape[1]
    adj_flat = adj32[...].astype(bf16)
    span = chunk * rank

    def merge(ch):
        cells = lax.broadcasted_iota(jnp.int32, (chunk * clusters, pairs), 0) + ch * (
            chunk * clusters
        )
        hot = jnp.where(cells == key, 1.0, 0.0).astype(bf16)
        cell = dot(hot, couplings[...])
        for t in range(chunk):
            tile = jnp.concatenate(
                [
                    cell[t * clusters : (t + 1) * clusters, a * block : (a + 1) * block]
                    for a in range(tall)
                ],
                axis=0,
            )
            turned = tile.T.astype(bf16)
            for i in range(group):
                merged[ch, t * rank : (t + 1) * rank, i * block : (i + 1) * block] = turned[
                    i * rank : (i + 1) * rank
                ]
        back = dot(merged[ch], adj_flat).astype(bf16)
        per = chunk // cap
        out_r[pl.ds(ch * per, per)] = back.reshape(per, cap, rank, block)

    loop(chunks, merge)
    loop(peers - 1, lambda step: far_copy(out_r, in_r, r_send, r_recv, step).start())
    in_r[me] = out_r[me]

    get_rows.wait()
    get_cols.wait()
    sorted_index(near_rows[...], near_cols[...], idx_v, 0)
    sorted_index(near_cols[...], near_rows[...], idx_v, 4)
    idx_copy = pltpu.make_async_copy(idx_v, idx, idx_sem)
    idx_copy.start()

    idx_copy.wait()
    for piece in get_near:
        piece.wait()
    segment_products(lambda b, t: dot(near[b], charges[t]), idx, 0, sums_f)
    for c in range(clusters):
        part_out[c] = sums_f[idx[3, other * clusters + c]].astype(bf16)
    pair_part = pltpu.make_async_remote_copy(
        src_ref=part_out,
        dst_ref=part_in,
        send_sem=pair_send.at[1],
        recv_sem=pair_recv.at[1],
        device_id={"sub": other},
        device_id_type=MESH,
    )
    pair_part.start()

    per = chunk // cap

    def placing(ch):
        lane = lax.broadcasted_iota(jnp.int32, (8, span), 1)
        target = jnp.full((8, span), -1, jnp.int32)
        for t in range(chunk):
            own = send[0, t % cap, ch * per + t // cap]
            target = jnp.where(lane // rank == t, own * rank + lane % rank, target)
        rows = lax.broadcasted_iota(jnp.int32, (clusters * rank, span), 0)
        place[ch] = jnp.where(rows == target[0:1], 1.0, 0.0).astype(bf16)

    loop(chunks, placing)

    pltpu.make_async_remote_copy(
        src_ref=loads_hbm,
        dst_ref=all_loads.at[pl.ds(other * clusters, clusters)],
        send_sem=pair_send.at[0],
        recv_sem=pair_recv.at[0],
        device_id={"sub": other},
        device_id_type=MESH,
    ).wait_recv()
    segment_products(lambda b, s: dot_t(near[b], all_loads[s]), idx, 4, sums_a)

    loop(peers - 1, lambda step: far_wait(out_f, in_f, f_send, f_recv, step).wait_recv())
    fwd32[...] = jnp.zeros(fwd32.shape, f32)

    def forward(ch):
        arrived = in_f[pl.ds(ch * per, per)].reshape(span, block)
        fwd32[...] += dot_t(arrived, merged[ch]).T

    loop(chunks, forward)

    for c in range(clusters):
        near_adj[c] = sums_a[idx[7, c]]
    pair_part.wait_recv()
    for c in range(clusters):
        far_c = fwd32[pl.ds(c, rank, stride=clusters), :].astype(bf16)
        far = dot_t(bases_perm[c], far_c)
        mine = sums_f[idx[3, core * clusters + c]]
        potentials[c] = (far + mine + part_in[c].astype(f32)).astype(bf16)

    loop(peers - 1, lambda step: far_wait(out_r, in_r, r_send, r_recv, step).wait_recv())
    total = jnp.zeros(adj32.shape, f32)
    if chunks == 1:
        total = dot(place[0], in_r[...].reshape(span, block))
    else:
        adj32[...] = total

        def scatter(ch):
            returned = in_r[pl.ds(ch * per, per)].reshape(span, block)
            adj32[...] += dot(place[ch], returned)

        loop(chunks, scatter)
        total = adj32[...]
    far_adj[...] = total.astype(bf16).reshape(clusters, rank, block)

    pair_loads.wait_send()
    pair_part.wait_send()
    loop(peers - 1, lambda step: far_wait(out_f, in_f, f_send, f_recv, step).wait_send())
    loop(peers - 1, lambda step: far_wait(out_r, in_r, r_send, r_recv, step).wait_send())


def finish(potentials, near_adj, far_adj, bases, potentials_hbm, adjoint_hbm, adjoint, sem):
    clusters = potentials.shape[0]
    size = clusters // PIECES
    copies = []

    def write(src, dst, piece, at):
        part = pl.ds(piece * size, size)
        copies.append(pltpu.make_async_copy(src.at[part], dst.at[part], sem.at[at]))
        copies[-1].start()

    for piece in range(PIECES):
        write(potentials, potentials_hbm, piece, piece)
    for piece in range(PIECES):
        for c in range(piece * size, (piece + 1) * size):
            adjoint[c] = (dot_t(bases[c], far_adj[c]) + near_adj[c]).astype(bf16)
        write(adjoint, adjoint_hbm, piece, PIECES + piece)
    for copy in copies:
        copy.wait()


def on_device(dims, *args):
    args = args[:-1] + (jnp.transpose(args[-1], (0, 2, 1)),)
    charges, loads, bases, couplings, near, near_rows, near_cols, far_rows, far_slots, send = args
    clusters, block, width = charges.shape
    rank = bases.shape[1]
    blocks = near.shape[0]
    cap, peers = send.shape[1], send.shape[2]
    chunk = min(CHUNK, peers * cap)
    vmem = pl.BlockSpec(memory_space=pltpu.VMEM)
    dma = pltpu.SemaphoreType.DMA
    slot_shape = (peers, cap, rank, width)
    full = jax.ShapeDtypeStruct((clusters, block, width), bf16)
    results = pl.pallas_call(
        functools.partial(kernel, dims),
        out_shape=(
            pltpu.VMEM(full.shape, bf16),
            pltpu.VMEM(full.shape, f32),
            pltpu.VMEM((clusters, rank, width), bf16),
            pltpu.VMEM(bases.shape, bf16),
        ),
        in_specs=[pl.BlockSpec(memory_space=pltpu.HBM)] * 10,
        out_specs=(vmem,) * 4,
        scratch_shapes=[
            pltpu.VMEM(charges.shape, bf16),
            pltpu.VMEM(couplings.shape, bf16),
            pltpu.VMEM(near.shape, bf16),
            pltpu.VMEM(near_rows.shape, jnp.int32),
            pltpu.VMEM(near_cols.shape, jnp.int32),
            pltpu.VMEM(far_rows.shape, jnp.int32),
            pltpu.VMEM(far_slots.shape, jnp.int32),
            pltpu.SMEM(send.shape, jnp.int32),
            pltpu.VMEM((8, 128), jnp.int32),
            pltpu.SMEM((8, 128), jnp.int32),
            pltpu.VMEM((clusters * rank, block), f32),
            pltpu.VMEM((clusters, rank, block), bf16),
            pltpu.VMEM((clusters, rank, width), bf16),
            pltpu.VMEM(slot_shape, bf16),
            pltpu.VMEM(slot_shape, bf16),
            pltpu.VMEM(slot_shape, bf16),
            pltpu.VMEM(slot_shape, bf16),
            pltpu.VMEM((clusters * rank, width), f32),
            pltpu.VMEM((peers * cap // chunk, chunk * rank, clusters * rank), bf16),
            pltpu.VMEM((peers * cap // chunk, clusters * rank, chunk * rank), bf16),
            pltpu.VMEM((clusters * rank, width), f32),
            pltpu.VMEM((blocks + 1, block, width), f32),
            pltpu.VMEM((blocks + 1, block, width), f32),
            pltpu.VMEM((2 * clusters, block, width), bf16),
            pltpu.VMEM((clusters, block, width), bf16),
            pltpu.VMEM((clusters, block, width), bf16),
            dma((10 + 2 * PIECES,)),
            dma,
            dma((peers,)),
            dma((peers,)),
            dma((peers,)),
            dma((peers,)),
            dma((2,)),
            dma((2,)),
        ],
        compiler_params=pltpu.CompilerParams(
            collective_id=0, has_side_effects=True, vmem_limit_bytes=54 * 1024 * 1024
        ),
        name="hierarchical",
    )(*args)
    return pl.pallas_call(
        finish,
        out_shape=(full, full),
        in_specs=[vmem] * 4,
        out_specs=(pl.BlockSpec(memory_space=pltpu.HBM),) * 2,
        scratch_shapes=[pltpu.VMEM(full.shape, bf16), dma((2 * PIECES,))],
        compiler_params=pltpu.CompilerParams(vmem_limit_bytes=4 * 1024 * 1024),
        name="finish",
    )(*results)


def solution(mesh):
    split = ("variant", "row", "col", "sub")
    owner = ("row", "col", "sub")
    in_specs = (
        P(split, None, None),
        P(split, None, None),
        P(split, None, None),
        P(split, None),
        P(split, None, None),
        P(owner, None),
        P(owner, None),
        P(owner, None),
        P(owner, None),
        P(owner, None, None),
    )
    out_specs = (P(split, None, None), P(split, None, None))
    return jax.shard_map(
        functools.partial(on_device, dict(mesh.shape)),
        mesh=mesh,
        in_specs=in_specs,
        out_specs=out_specs,
        check_vma=False,
    )
```

```python
import functools

import jax
import jax.numpy as jnp
from jax import lax
from jax.experimental import pallas as pl
from jax.experimental.pallas import tpu as pltpu
from jax.sharding import PartitionSpec as P

MESH = pl.DeviceIdType.MESH
f32 = jnp.float32
bf16 = jnp.bfloat16
UNROLL = 8
CHUNK = 16
PIECES = 2


def loop(count, body):
    if count <= 16:
        for step in range(count):
            body(step)
    else:

        def step_body(step, carry):
            body(step)
            return carry

        lax.fori_loop(0, count, step_body, 0)


def dot(a, b):
    return jnp.dot(a, b, preferred_element_type=f32)


def dot_t(a, b):
    return lax.dot_general(a, b, (((0,), (0,)), ((), ())), preferred_element_type=f32)


def sorted_index(keys_row, other_row, idx_ref, at):
    n = keys_row.shape[1]
    lane = lax.broadcasted_iota(jnp.int32, (n, n), 1)
    sub = lax.broadcasted_iota(jnp.int32, (n, n), 0)
    keys = jnp.broadcast_to(keys_row, (n, n))
    eye = lane == sub
    key_col = jnp.sum(jnp.where(eye, keys, 0), axis=1, keepdims=True)
    other_col = jnp.sum(
        jnp.where(eye, jnp.broadcast_to(other_row, (n, n)), 0), axis=1, keepdims=True
    )
    before = (keys < key_col) | ((keys == key_col) & (lane < sub))
    rank = jnp.sum(jnp.where(before, 1, 0), axis=1, keepdims=True)
    wide = (n, 128)
    lanes = lax.broadcasted_iota(jnp.int32, wide, 1)
    subs = lax.broadcasted_iota(jnp.int32, wide, 0)
    here = rank == lanes

    def pick(values):
        return jnp.sum(jnp.where(here, values, 0), axis=0, keepdims=True)

    idx_ref[at : at + 1, :] = pick(subs)
    idx_ref[at + 1 : at + 2, :] = pick(jnp.broadcast_to(key_col, wide))
    idx_ref[at + 2 : at + 3, :] = pick(jnp.broadcast_to(other_col, wide))
    upto = jnp.sum(jnp.where(key_col <= lanes, 1, 0), axis=0, keepdims=True)
    same = jnp.sum(jnp.where(key_col == lanes, 1, 0), axis=0, keepdims=True)
    idx_ref[at + 3 : at + 4, :] = jnp.where(same > 0, upto - 1, n)


def segment_products(product, idx, at, sums):
    n = sums.shape[0] - 1
    unroll = UNROLL if n % UNROLL == 0 else 1
    sums[n] = jnp.zeros(sums.shape[1:], f32)

    def body(step, total):
        terms = []
        for u in range(unroll):
            k = step * unroll + u
            terms.append(product(idx[at, k], idx[at + 2, k]))
        for u in range(unroll):
            k = step * unroll + u
            same = (idx[at + 1, k] == idx[at + 1, jnp.maximum(k - 1, 0)]) & (k > 0)
            total = total * jnp.where(same, 1.0, 0.0).astype(f32) + terms[u]
            sums[k] = total
        return total

    lax.fori_loop(0, n // unroll, body, jnp.zeros(sums.shape[1:], f32))


def kernel(
    dims,
    charges_hbm,
    loads_hbm,
    bases_hbm,
    couplings_hbm,
    near_hbm,
    near_rows_hbm,
    near_cols_hbm,
    far_rows_hbm,
    far_slots_hbm,
    send_hbm,
    potentials,
    near_adj,
    far_adj,
    bases,
    charges,
    couplings,
    near,
    near_rows,
    near_cols,
    far_rows,
    far_slots,
    send,
    idx_v,
    idx,
    bases32,
    bases_perm,
    coeffs,
    out_f,
    in_f,
    out_r,
    in_r,
    adj32,
    merged,
    place,
    fwd32,
    sums_f,
    sums_a,
    all_loads,
    part_out,
    part_in,
    in_sem,
    idx_sem,
    f_send,
    f_recv,
    r_send,
    r_recv,
    pair_send,
    pair_recv,
):
    cols = dims["col"]
    clusters, rank, block = bases.shape
    cap, peers = send.shape[1], send.shape[2]
    slots = peers * cap
    chunk = min(CHUNK, slots)
    chunks = slots // chunk
    group = block // rank
    tall = rank // group
    row, col, core = lax.axis_index("row"), lax.axis_index("col"), lax.axis_index("sub")
    me = row * cols + col
    other = 1 - core

    def peer_of(d):
        if peers & (peers - 1):
            p = lax.rem(me + d, peers)
        else:
            p, bit = 0, 1
            while bit < peers:
                p = p + lax.rem(me // bit + (peers - d) // bit, 2) * bit
                bit *= 2
        return p, {"row": p // cols, "col": lax.rem(p, cols)}

    def fetch(src, dst, at):
        copy = pltpu.make_async_copy(src, dst, in_sem.at[at])
        copy.start()
        return copy

    def fetch_pieces(src, dst, at):
        size = src.shape[0] // PIECES
        return [
            fetch(src.at[pl.ds(i * size, size)], dst.at[pl.ds(i * size, size)], at + i)
            for i in range(PIECES)
        ]

    get_bases = fetch(bases_hbm, bases, 0)
    get_charges = fetch_pieces(charges_hbm, charges, 10)
    barrier = pltpu.get_barrier_semaphore()
    pl.semaphore_signal(barrier, inc=1, device_id={"sub": other}, device_id_type=MESH)

    def greet(step):
        _, device = peer_of(step + 1)
        pl.semaphore_signal(barrier, inc=1, device_id=device, device_id_type=MESH)

    loop(peers - 1, greet)

    get_send = fetch(send_hbm, send, 2)
    get_loads = fetch(loads_hbm, all_loads.at[pl.ds(core * clusters, clusters)], 3)
    get_bases.wait()
    for c in range(clusters):
        if c % (clusters // PIECES) == 0:
            get_charges[c // (clusters // PIECES)].wait()
        coeffs[c] = dot(bases[c], charges[c]).astype(bf16)
    get_send.wait()

    def fill(p):
        for k in range(cap):
            out_f[p, k] = coeffs[jnp.maximum(send[0, k, p], 0)]

    loop(peers, fill)
    pl.semaphore_wait(barrier, peers)

    def far_copy(src, dst, send_sem, recv_sem, step):
        p, device = peer_of(step + 1)
        return pltpu.make_async_remote_copy(
            src_ref=src.at[p],
            dst_ref=dst.at[me],
            send_sem=send_sem.at[p],
            recv_sem=recv_sem.at[me],
            device_id=device,
            device_id_type=MESH,
        )

    def far_wait(src, dst, send_sem, recv_sem, step):
        p, device = peer_of(step + 1)
        return pltpu.make_async_remote_copy(
            src_ref=src.at[p],
            dst_ref=dst.at[p],
            send_sem=send_sem.at[p],
            recv_sem=recv_sem.at[p],
            device_id=device,
            device_id_type=MESH,
        )

    loop(peers - 1, lambda step: far_copy(out_f, in_f, f_send, f_recv, step).start())
    get_couplings = fetch(couplings_hbm, couplings, 4)
    get_far_rows = fetch(far_rows_hbm, far_rows, 5)
    get_far_slots = fetch(far_slots_hbm, far_slots, 6)
    get_rows = fetch(near_rows_hbm, near_rows, 7)
    get_cols = fetch(near_cols_hbm, near_cols, 8)
    get_near = fetch_pieces(near_hbm, near, 10 + PIECES)

    in_f[me] = out_f[me]
    pair_loads = pltpu.make_async_remote_copy(
        src_ref=loads_hbm,
        dst_ref=all_loads.at[pl.ds(core * clusters, clusters)],
        send_sem=pair_send.at[0],
        recv_sem=pair_recv.at[0],
        device_id={"sub": other},
        device_id_type=MESH,
    )
    pair_loads.start()

    get_loads.wait()
    bases32[...] = bases[...].astype(f32).reshape(clusters * rank, block)
    for c in range(clusters):
        parts = [bases32[pl.ds(c * rank + i, tall, stride=group), :] for i in range(group)]
        bases_perm[c] = jnp.concatenate(parts, axis=0).astype(bf16)
        adj32[pl.ds(c, rank, stride=clusters), :] = dot(
            bases_perm[c], all_loads[core * clusters + c]
        )

    get_far_rows.wait()
    get_far_slots.wait()
    get_couplings.wait()
    key = far_slots[...] * clusters + far_rows[...]
    pairs = key.shape[1]
    adj_flat = adj32[...].astype(bf16)
    span = chunk * rank

    def merge(ch):
        cells = lax.broadcasted_iota(jnp.int32, (chunk * clusters, pairs), 0) + ch * (
            chunk * clusters
        )
        hot = jnp.where(cells == key, 1.0, 0.0).astype(bf16)
        cell = dot(hot, couplings[...])
        for t in range(chunk):
            tile = jnp.concatenate(
                [
                    cell[t * clusters : (t + 1) * clusters, a * block : (a + 1) * block]
                    for a in range(tall)
                ],
                axis=0,
            )
            turned = tile.T.astype(bf16)
            for i in range(group):
                merged[ch, t * rank : (t + 1) * rank, i * block : (i + 1) * block] = turned[
                    i * rank : (i + 1) * rank
                ]
        back = dot(merged[ch], adj_flat).astype(bf16)
        per = chunk // cap
        out_r[pl.ds(ch * per, per)] = back.reshape(per, cap, rank, block)

    loop(chunks, merge)
    loop(peers - 1, lambda step: far_copy(out_r, in_r, r_send, r_recv, step).start())
    in_r[me] = out_r[me]

    get_rows.wait()
    get_cols.wait()
    sorted_index(near_rows[...], near_cols[...], idx_v, 0)
    sorted_index(near_cols[...], near_rows[...], idx_v, 4)
    idx_copy = pltpu.make_async_copy(idx_v, idx, idx_sem)
    idx_copy.start()

    idx_copy.wait()
    for piece in get_near:
        piece.wait()
    segment_products(lambda b, t: dot(near[b], charges[t]), idx, 0, sums_f)
    for c in range(clusters):
        part_out[c] = sums_f[idx[3, other * clusters + c]].astype(bf16)
    pair_part = pltpu.make_async_remote_copy(
        src_ref=part_out,
        dst_ref=part_in,
        send_sem=pair_send.at[1],
        recv_sem=pair_recv.at[1],
        device_id={"sub": other},
        device_id_type=MESH,
    )
    pair_part.start()

    per = chunk // cap

    def placing(ch):
        lane = lax.broadcasted_iota(jnp.int32, (8, span), 1)
        target = jnp.full((8, span), -1, jnp.int32)
        for t in range(chunk):
            own = send[0, t % cap, ch * per + t // cap]
            target = jnp.where(lane // rank == t, own * rank + lane % rank, target)
        rows = lax.broadcasted_iota(jnp.int32, (clusters * rank, span), 0)
        place[ch] = jnp.where(rows == target[0:1], 1.0, 0.0).astype(bf16)

    loop(chunks, placing)

    pltpu.make_async_remote_copy(
        src_ref=loads_hbm,
        dst_ref=all_loads.at[pl.ds(other * clusters, clusters)],
        send_sem=pair_send.at[0],
        recv_sem=pair_recv.at[0],
        device_id={"sub": other},
        device_id_type=MESH,
    ).wait_recv()
    segment_products(lambda b, s: dot_t(near[b], all_loads[s]), idx, 4, sums_a)

    loop(peers - 1, lambda step: far_wait(out_f, in_f, f_send, f_recv, step).wait_recv())
    fwd32[...] = jnp.zeros(fwd32.shape, f32)

    def forward(ch):
        arrived = in_f[pl.ds(ch * per, per)].reshape(span, block)
        fwd32[...] += dot_t(arrived, merged[ch]).T

    loop(chunks, forward)

    for c in range(clusters):
        near_adj[c] = sums_a[idx[7, c]]
    pair_part.wait_recv()
    for c in range(clusters):
        far_c = fwd32[pl.ds(c, rank, stride=clusters), :].astype(bf16)
        far = dot_t(bases_perm[c], far_c)
        mine = sums_f[idx[3, core * clusters + c]]
        potentials[c] = (far + mine + part_in[c].astype(f32)).astype(bf16)

    loop(peers - 1, lambda step: far_wait(out_r, in_r, r_send, r_recv, step).wait_recv())
    total = jnp.zeros(adj32.shape, f32)
    if chunks == 1:
        total = dot(place[0], in_r[...].reshape(span, block))
    else:
        adj32[...] = total

        def scatter(ch):
            returned = in_r[pl.ds(ch * per, per)].reshape(span, block)
            adj32[...] += dot(place[ch], returned)

        loop(chunks, scatter)
        total = adj32[...]
    far_adj[...] = total.astype(bf16).reshape(clusters, rank, block)

    pair_loads.wait_send()
    pair_part.wait_send()
    loop(peers - 1, lambda step: far_wait(out_f, in_f, f_send, f_recv, step).wait_send())
    loop(peers - 1, lambda step: far_wait(out_r, in_r, r_send, r_recv, step).wait_send())


def finish(potentials, near_adj, far_adj, bases, potentials_hbm, adjoint_hbm, adjoint, sem):
    clusters = potentials.shape[0]
    size = clusters // PIECES
    copies = []

    def write(src, dst, piece, at):
        part = pl.ds(piece * size, size)
        copies.append(pltpu.make_async_copy(src.at[part], dst.at[part], sem.at[at]))
        copies[-1].start()

    for piece in range(PIECES):
        write(potentials, potentials_hbm, piece, piece)
    for piece in range(PIECES):
        for c in range(piece * size, (piece + 1) * size):
            adjoint[c] = (dot_t(bases[c], far_adj[c]) + near_adj[c]).astype(bf16)
        write(adjoint, adjoint_hbm, piece, PIECES + piece)
    for copy in copies:
        copy.wait()


def on_device(dims, *args):
    args = args[:-1] + (jnp.transpose(args[-1], (0, 2, 1)),)
    charges, loads, bases, couplings, near, near_rows, near_cols, far_rows, far_slots, send = args
    clusters, block, width = charges.shape
    rank = bases.shape[1]
    blocks = near.shape[0]
    cap, peers = send.shape[1], send.shape[2]
    chunk = min(CHUNK, peers * cap)
    vmem = pl.BlockSpec(memory_space=pltpu.VMEM)
    dma = pltpu.SemaphoreType.DMA
    slot_shape = (peers, cap, rank, width)
    full = jax.ShapeDtypeStruct((clusters, block, width), bf16)
    results = pl.pallas_call(
        functools.partial(kernel, dims),
        out_shape=(
            pltpu.VMEM(full.shape, bf16),
            pltpu.VMEM(full.shape, f32),
            pltpu.VMEM((clusters, rank, width), bf16),
            pltpu.VMEM(bases.shape, bf16),
        ),
        in_specs=[pl.BlockSpec(memory_space=pltpu.HBM)] * 10,
        out_specs=(vmem,) * 4,
        scratch_shapes=[
            pltpu.VMEM(charges.shape, bf16),
            pltpu.VMEM(couplings.shape, bf16),
            pltpu.VMEM(near.shape, bf16),
            pltpu.VMEM(near_rows.shape, jnp.int32),
            pltpu.VMEM(near_cols.shape, jnp.int32),
            pltpu.VMEM(far_rows.shape, jnp.int32),
            pltpu.VMEM(far_slots.shape, jnp.int32),
            pltpu.SMEM(send.shape, jnp.int32),
            pltpu.VMEM((8, 128), jnp.int32),
            pltpu.SMEM((8, 128), jnp.int32),
            pltpu.VMEM((clusters * rank, block), f32),
            pltpu.VMEM((clusters, rank, block), bf16),
            pltpu.VMEM((clusters, rank, width), bf16),
            pltpu.VMEM(slot_shape, bf16),
            pltpu.VMEM(slot_shape, bf16),
            pltpu.VMEM(slot_shape, bf16),
            pltpu.VMEM(slot_shape, bf16),
            pltpu.VMEM((clusters * rank, width), f32),
            pltpu.VMEM((peers * cap // chunk, chunk * rank, clusters * rank), bf16),
            pltpu.VMEM((peers * cap // chunk, clusters * rank, chunk * rank), bf16),
            pltpu.VMEM((clusters * rank, width), f32),
            pltpu.VMEM((blocks + 1, block, width), f32),
            pltpu.VMEM((blocks + 1, block, width), f32),
            pltpu.VMEM((2 * clusters, block, width), bf16),
            pltpu.VMEM((clusters, block, width), bf16),
            pltpu.VMEM((clusters, block, width), bf16),
            dma((10 + 2 * PIECES,)),
            dma,
            dma((peers,)),
            dma((peers,)),
            dma((peers,)),
            dma((peers,)),
            dma((2,)),
            dma((2,)),
        ],
        compiler_params=pltpu.CompilerParams(
            collective_id=0, has_side_effects=True, vmem_limit_bytes=54 * 1024 * 1024
        ),
        name="hierarchical",
    )(*args)
    return pl.pallas_call(
        finish,
        out_shape=(full, full),
        in_specs=[vmem] * 4,
        out_specs=(pl.BlockSpec(memory_space=pltpu.HBM),) * 2,
        scratch_shapes=[pltpu.VMEM(full.shape, bf16), dma((2 * PIECES,))],
        compiler_params=pltpu.CompilerParams(vmem_limit_bytes=4 * 1024 * 1024),
        name="finish",
    )(*results)


def solution(mesh):
    split = ("variant", "row", "col", "sub")
    owner = ("row", "col", "sub")
    in_specs = (
        P(split, None, None),
        P(split, None, None),
        P(split, None, None),
        P(split, None),
        P(split, None, None),
        P(owner, None),
        P(owner, None),
        P(owner, None),
        P(owner, None),
        P(owner, None, None),
    )
    out_specs = (P(split, None, None), P(split, None, None))
    return jax.shard_map(
        functools.partial(on_device, dict(mesh.shape)),
        mesh=mesh,
        in_specs=in_specs,
        out_specs=out_specs,
        check_vma=False,
    )
```

```python
import functools

import jax
import jax.numpy as jnp
from jax import lax
from jax.experimental import pallas as pl
from jax.experimental.pallas import tpu as pltpu
from jax.sharding import PartitionSpec as P

MESH = pl.DeviceIdType.MESH
f32 = jnp.float32
bf16 = jnp.bfloat16
UNROLL = 8
CHUNK = 16
PIECES = 2


def loop(count, body):
    if count <= 16:
        for step in range(count):
            body(step)
    else:

        def step_body(step, carry):
            body(step)
            return carry

        lax.fori_loop(0, count, step_body, 0)


def dot(a, b):
    return jnp.dot(a, b, preferred_element_type=f32)


def dot_t(a, b):
    return lax.dot_general(a, b, (((0,), (0,)), ((), ())), preferred_element_type=f32)


def sorted_index(keys_row, other_row, idx_ref, at):
    n = keys_row.shape[1]
    lane = lax.broadcasted_iota(jnp.int32, (n, n), 1)
    sub = lax.broadcasted_iota(jnp.int32, (n, n), 0)
    keys = jnp.broadcast_to(keys_row, (n, n))
    eye = lane == sub
    key_col = jnp.sum(jnp.where(eye, keys, 0), axis=1, keepdims=True)
    other_col = jnp.sum(
        jnp.where(eye, jnp.broadcast_to(other_row, (n, n)), 0), axis=1, keepdims=True
    )
    before = (keys < key_col) | ((keys == key_col) & (lane < sub))
    rank = jnp.sum(jnp.where(before, 1, 0), axis=1, keepdims=True)
    wide = (n, 128)
    lanes = lax.broadcasted_iota(jnp.int32, wide, 1)
    subs = lax.broadcasted_iota(jnp.int32, wide, 0)
    here = rank == lanes

    def pick(values):
        return jnp.sum(jnp.where(here, values, 0), axis=0, keepdims=True)

    idx_ref[at : at + 1, :] = pick(subs)
    idx_ref[at + 1 : at + 2, :] = pick(jnp.broadcast_to(key_col, wide))
    idx_ref[at + 2 : at + 3, :] = pick(jnp.broadcast_to(other_col, wide))
    upto = jnp.sum(jnp.where(key_col <= lanes, 1, 0), axis=0, keepdims=True)
    same = jnp.sum(jnp.where(key_col == lanes, 1, 0), axis=0, keepdims=True)
    idx_ref[at + 3 : at + 4, :] = jnp.where(same > 0, upto - 1, n)


def segment_products(product, idx, at, sums):
    n = sums.shape[0] - 1
    unroll = UNROLL if n % UNROLL == 0 else 1
    sums[n] = jnp.zeros(sums.shape[1:], f32)

    def body(step, total):
        terms = []
        for u in range(unroll):
            k = step * unroll + u
            terms.append(product(idx[at, k], idx[at + 2, k]))
        for u in range(unroll):
            k = step * unroll + u
            same = (idx[at + 1, k] == idx[at + 1, jnp.maximum(k - 1, 0)]) & (k > 0)
            total = total * jnp.where(same, 1.0, 0.0).astype(f32) + terms[u]
            sums[k] = total
        return total

    lax.fori_loop(0, n // unroll, body, jnp.zeros(sums.shape[1:], f32))


def kernel(
    dims,
    charges_hbm,
    loads_hbm,
    bases_hbm,
    couplings_hbm,
    near_hbm,
    near_rows_hbm,
    near_cols_hbm,
    far_rows_hbm,
    far_slots_hbm,
    send_hbm,
    potentials,
    near_adj,
    far_adj,
    bases,
    charges,
    couplings,
    near,
    near_rows,
    near_cols,
    far_rows,
    far_slots,
    send,
    idx_v,
    idx,
    bases32,
    bases_perm,
    coeffs,
    out_f,
    in_f,
    out_r,
    in_r,
    adj32,
    merged,
    place,
    fwd32,
    sums_f,
    sums_a,
    all_loads,
    part_out,
    part_in,
    in_sem,
    idx_sem,
    f_send,
    f_recv,
    r_send,
    r_recv,
    pair_send,
    pair_recv,
):
    cols = dims["col"]
    clusters, rank, block = bases.shape
    cap, peers = send.shape[1], send.shape[2]
    slots = peers * cap
    chunk = min(CHUNK, slots)
    chunks = slots // chunk
    group = block // rank
    tall = rank // group
    row, col, core = lax.axis_index("row"), lax.axis_index("col"), lax.axis_index("sub")
    me = row * cols + col
    other = 1 - core

    def peer_of(d):
        if peers & (peers - 1):
            p = lax.rem(me + d, peers)
        else:
            p, bit = 0, 1
            while bit < peers:
                p = p + lax.rem(me // bit + (peers - d) // bit, 2) * bit
                bit *= 2
        return p, {"row": p // cols, "col": lax.rem(p, cols)}

    def fetch(src, dst, at):
        copy = pltpu.make_async_copy(src, dst, in_sem.at[at])
        copy.start()
        return copy

    def fetch_pieces(src, dst, at):
        size = src.shape[0] // PIECES
        return [
            fetch(src.at[pl.ds(i * size, size)], dst.at[pl.ds(i * size, size)], at + i)
            for i in range(PIECES)
        ]

    get_bases = fetch(bases_hbm, bases, 0)
    get_charges = fetch_pieces(charges_hbm, charges, 10)
    barrier = pltpu.get_barrier_semaphore()
    pl.semaphore_signal(barrier, inc=1, device_id={"sub": other}, device_id_type=MESH)

    def greet(step):
        _, device = peer_of(step + 1)
        pl.semaphore_signal(barrier, inc=1, device_id=device, device_id_type=MESH)

    loop(peers - 1, greet)

    get_send = fetch(send_hbm, send, 2)
    get_loads = fetch(loads_hbm, all_loads.at[pl.ds(core * clusters, clusters)], 3)
    get_bases.wait()
    for c in range(clusters):
        if c % (clusters // PIECES) == 0:
            get_charges[c // (clusters // PIECES)].wait()
        coeffs[c] = dot(bases[c], charges[c]).astype(bf16)
    get_send.wait()

    def fill(p):
        for k in range(cap):
            out_f[p, k] = coeffs[jnp.maximum(send[0, k, p], 0)]

    loop(peers, fill)
    pl.semaphore_wait(barrier, peers)

    def far_copy(src, dst, send_sem, recv_sem, step):
        p, device = peer_of(step + 1)
        return pltpu.make_async_remote_copy(
            src_ref=src.at[p],
            dst_ref=dst.at[me],
            send_sem=send_sem.at[p],
            recv_sem=recv_sem.at[me],
            device_id=device,
            device_id_type=MESH,
        )

    def far_wait(src, dst, send_sem, recv_sem, step):
        p, device = peer_of(step + 1)
        return pltpu.make_async_remote_copy(
            src_ref=src.at[p],
            dst_ref=dst.at[p],
            send_sem=send_sem.at[p],
            recv_sem=recv_sem.at[p],
            device_id=device,
            device_id_type=MESH,
        )

    loop(peers - 1, lambda step: far_copy(out_f, in_f, f_send, f_recv, step).start())
    get_couplings = fetch(couplings_hbm, couplings, 4)
    get_far_rows = fetch(far_rows_hbm, far_rows, 5)
    get_far_slots = fetch(far_slots_hbm, far_slots, 6)
    get_rows = fetch(near_rows_hbm, near_rows, 7)
    get_cols = fetch(near_cols_hbm, near_cols, 8)
    get_near = [fetch(near_hbm, near, 10 + PIECES)]

    in_f[me] = out_f[me]
    get_loads.wait()
    bases32[...] = bases[...].astype(f32).reshape(clusters * rank, block)
    for c in range(clusters):
        parts = [bases32[pl.ds(c * rank + i, tall, stride=group), :] for i in range(group)]
        bases_perm[c] = jnp.concatenate(parts, axis=0).astype(bf16)
        adj32[pl.ds(c, rank, stride=clusters), :] = dot(
            bases_perm[c], all_loads[core * clusters + c]
        )

    get_far_rows.wait()
    get_far_slots.wait()
    get_couplings.wait()
    key = far_slots[...] * clusters + far_rows[...]
    pairs = key.shape[1]
    adj_flat = adj32[...].astype(bf16)
    span = chunk * rank

    def merge(ch):
        cells = lax.broadcasted_iota(jnp.int32, (chunk * clusters, pairs), 0) + ch * (
            chunk * clusters
        )
        hot = jnp.where(cells == key, 1.0, 0.0).astype(bf16)
        cell = dot(hot, couplings[...])
        for t in range(chunk):
            tile = jnp.concatenate(
                [
                    cell[t * clusters : (t + 1) * clusters, a * block : (a + 1) * block]
                    for a in range(tall)
                ],
                axis=0,
            )
            turned = tile.T.astype(bf16)
            for i in range(group):
                merged[ch, t * rank : (t + 1) * rank, i * block : (i + 1) * block] = turned[
                    i * rank : (i + 1) * rank
                ]
        back = dot(merged[ch], adj_flat).astype(bf16)
        per = chunk // cap
        out_r[pl.ds(ch * per, per)] = back.reshape(per, cap, rank, block)

    loop(chunks, merge)
    loop(peers - 1, lambda step: far_copy(out_r, in_r, r_send, r_recv, step).start())
    pair_loads = pltpu.make_async_remote_copy(
        src_ref=loads_hbm,
        dst_ref=all_loads.at[pl.ds(core * clusters, clusters)],
        send_sem=pair_send.at[0],
        recv_sem=pair_recv.at[0],
        device_id={"sub": other},
        device_id_type=MESH,
    )
    pair_loads.start()
    in_r[me] = out_r[me]

    get_rows.wait()
    get_cols.wait()
    sorted_index(near_rows[...], near_cols[...], idx_v, 0)
    sorted_index(near_cols[...], near_rows[...], idx_v, 4)
    idx_copy = pltpu.make_async_copy(idx_v, idx, idx_sem)
    idx_copy.start()

    idx_copy.wait()
    for piece in get_near:
        piece.wait()
    segment_products(lambda b, t: dot(near[b], charges[t]), idx, 0, sums_f)
    for c in range(clusters):
        part_out[c] = sums_f[idx[3, other * clusters + c]].astype(bf16)
    pair_part = pltpu.make_async_remote_copy(
        src_ref=part_out,
        dst_ref=part_in,
        send_sem=pair_send.at[1],
        recv_sem=pair_recv.at[1],
        device_id={"sub": other},
        device_id_type=MESH,
    )
    pair_part.start()

    per = chunk // cap

    def placing(ch):
        lane = lax.broadcasted_iota(jnp.int32, (8, span), 1)
        target = jnp.full((8, span), -1, jnp.int32)
        for t in range(chunk):
            own = send[0, t % cap, ch * per + t // cap]
            target = jnp.where(lane // rank == t, own * rank + lane % rank, target)
        rows = lax.broadcasted_iota(jnp.int32, (clusters * rank, span), 0)
        place[ch] = jnp.where(rows == target[0:1], 1.0, 0.0).astype(bf16)

    loop(chunks, placing)

    pltpu.make_async_remote_copy(
        src_ref=loads_hbm,
        dst_ref=all_loads.at[pl.ds(other * clusters, clusters)],
        send_sem=pair_send.at[0],
        recv_sem=pair_recv.at[0],
        device_id={"sub": other},
        device_id_type=MESH,
    ).wait_recv()
    segment_products(lambda b, s: dot_t(near[b], all_loads[s]), idx, 4, sums_a)

    loop(peers - 1, lambda step: far_wait(out_f, in_f, f_send, f_recv, step).wait_recv())
    fwd32[...] = jnp.zeros(fwd32.shape, f32)

    def forward(ch):
        arrived = in_f[pl.ds(ch * per, per)].reshape(span, block)
        fwd32[...] += dot_t(arrived, merged[ch]).T

    loop(chunks, forward)

    for c in range(clusters):
        near_adj[c] = sums_a[idx[7, c]]
    pair_part.wait_recv()
    for c in range(clusters):
        far_c = fwd32[pl.ds(c, rank, stride=clusters), :].astype(bf16)
        far = dot_t(bases_perm[c], far_c)
        mine = sums_f[idx[3, core * clusters + c]]
        potentials[c] = (far + mine + part_in[c].astype(f32)).astype(bf16)

    loop(peers - 1, lambda step: far_wait(out_r, in_r, r_send, r_recv, step).wait_recv())
    total = jnp.zeros(adj32.shape, f32)
    if chunks == 1:
        total = dot(place[0], in_r[...].reshape(span, block))
    else:
        adj32[...] = total

        def scatter(ch):
            returned = in_r[pl.ds(ch * per, per)].reshape(span, block)
            adj32[...] += dot(place[ch], returned)

        loop(chunks, scatter)
        total = adj32[...]
    far_adj[...] = total.astype(bf16).reshape(clusters, rank, block)

    pair_loads.wait_send()
    pair_part.wait_send()
    loop(peers - 1, lambda step: far_wait(out_f, in_f, f_send, f_recv, step).wait_send())
    loop(peers - 1, lambda step: far_wait(out_r, in_r, r_send, r_recv, step).wait_send())


def finish(potentials, near_adj, far_adj, bases, potentials_hbm, adjoint_hbm, adjoint, sem):
    clusters = potentials.shape[0]
    size = clusters // PIECES
    copies = []

    def write(src, dst, piece, at):
        part = pl.ds(piece * size, size)
        copies.append(pltpu.make_async_copy(src.at[part], dst.at[part], sem.at[at]))
        copies[-1].start()

    for piece in range(PIECES):
        write(potentials, potentials_hbm, piece, piece)
    for piece in range(PIECES):
        for c in range(piece * size, (piece + 1) * size):
            adjoint[c] = (dot_t(bases[c], far_adj[c]) + near_adj[c]).astype(bf16)
        write(adjoint, adjoint_hbm, piece, PIECES + piece)
    for copy in copies:
        copy.wait()


def on_device(dims, *args):
    args = args[:-1] + (jnp.transpose(args[-1], (0, 2, 1)),)
    charges, loads, bases, couplings, near, near_rows, near_cols, far_rows, far_slots, send = args
    clusters, block, width = charges.shape
    rank = bases.shape[1]
    blocks = near.shape[0]
    cap, peers = send.shape[1], send.shape[2]
    chunk = min(CHUNK, peers * cap)
    vmem = pl.BlockSpec(memory_space=pltpu.VMEM)
    dma = pltpu.SemaphoreType.DMA
    slot_shape = (peers, cap, rank, width)
    full = jax.ShapeDtypeStruct((clusters, block, width), bf16)
    results = pl.pallas_call(
        functools.partial(kernel, dims),
        out_shape=(
            pltpu.VMEM(full.shape, bf16),
            pltpu.VMEM(full.shape, f32),
            pltpu.VMEM((clusters, rank, width), bf16),
            pltpu.VMEM(bases.shape, bf16),
        ),
        in_specs=[pl.BlockSpec(memory_space=pltpu.HBM)] * 10,
        out_specs=(vmem,) * 4,
        scratch_shapes=[
            pltpu.VMEM(charges.shape, bf16),
            pltpu.VMEM(couplings.shape, bf16),
            pltpu.VMEM(near.shape, bf16),
            pltpu.VMEM(near_rows.shape, jnp.int32),
            pltpu.VMEM(near_cols.shape, jnp.int32),
            pltpu.VMEM(far_rows.shape, jnp.int32),
            pltpu.VMEM(far_slots.shape, jnp.int32),
            pltpu.SMEM(send.shape, jnp.int32),
            pltpu.VMEM((8, 128), jnp.int32),
            pltpu.SMEM((8, 128), jnp.int32),
            pltpu.VMEM((clusters * rank, block), f32),
            pltpu.VMEM((clusters, rank, block), bf16),
            pltpu.VMEM((clusters, rank, width), bf16),
            pltpu.VMEM(slot_shape, bf16),
            pltpu.VMEM(slot_shape, bf16),
            pltpu.VMEM(slot_shape, bf16),
            pltpu.VMEM(slot_shape, bf16),
            pltpu.VMEM((clusters * rank, width), f32),
            pltpu.VMEM((peers * cap // chunk, chunk * rank, clusters * rank), bf16),
            pltpu.VMEM((peers * cap // chunk, clusters * rank, chunk * rank), bf16),
            pltpu.VMEM((clusters * rank, width), f32),
            pltpu.VMEM((blocks + 1, block, width), f32),
            pltpu.VMEM((blocks + 1, block, width), f32),
            pltpu.VMEM((2 * clusters, block, width), bf16),
            pltpu.VMEM((clusters, block, width), bf16),
            pltpu.VMEM((clusters, block, width), bf16),
            dma((10 + 2 * PIECES,)),
            dma,
            dma((peers,)),
            dma((peers,)),
            dma((peers,)),
            dma((peers,)),
            dma((2,)),
            dma((2,)),
        ],
        compiler_params=pltpu.CompilerParams(
            collective_id=0, has_side_effects=True, vmem_limit_bytes=54 * 1024 * 1024
        ),
        name="hierarchical",
    )(*args)
    return pl.pallas_call(
        finish,
        out_shape=(full, full),
        in_specs=[vmem] * 4,
        out_specs=(pl.BlockSpec(memory_space=pltpu.HBM),) * 2,
        scratch_shapes=[pltpu.VMEM(full.shape, bf16), dma((2 * PIECES,))],
        compiler_params=pltpu.CompilerParams(vmem_limit_bytes=4 * 1024 * 1024),
        name="finish",
    )(*results)


def solution(mesh):
    split = ("variant", "row", "col", "sub")
    owner = ("row", "col", "sub")
    in_specs = (
        P(split, None, None),
        P(split, None, None),
        P(split, None, None),
        P(split, None),
        P(split, None, None),
        P(owner, None),
        P(owner, None),
        P(owner, None),
        P(owner, None),
        P(owner, None, None),
    )
    out_specs = (P(split, None, None), P(split, None, None))
    return jax.shard_map(
        functools.partial(on_device, dict(mesh.shape)),
        mesh=mesh,
        in_specs=in_specs,
        out_specs=out_specs,
        check_vma=False,
    )
```
